256 devices in a mesh: grp: 8 (over z), seq: 16 (over y, x), resp: 2 (over core).
Axes of the slice: x: 4, y: 4, z: 8, core: 2. Of those that a mesh axis runs over, the one named last changes fastest.
Arguments:
- prompt_xbc: bfloat16 [65536, 5376], P(('grp', 'seq', 'resp')), parts along dimension 0, may hold values from -6 to 6
- prompt_z: bfloat16 [65536, 5120], P(('grp', 'seq', 'resp')), parts along dimension 0, may hold values from -6 to 6
- prompt_step: float32 [80, 65536], P(None, ('grp', 'seq', 'resp')), parts along dimension 1, may hold values from 0 to 0.2
- prompt_keep: float32 [80, 65536], P(None, ('grp', 'seq', 'resp')), parts along dimension 1, may hold values from -0.6 to 0
- resp_xbc: bfloat16 [256, 128, 5376], P(('grp', 'seq', 'resp')), parts along dimension 0, may hold values from -6 to 6
- resp_z: bfloat16 [256, 128, 5120], P(('grp', 'seq', 'resp')), parts along dimension 0, may hold values from -6 to 6
- resp_step: float32 [80, 256, 128], P(None, ('grp', 'seq', 'resp')), parts along dimension 1, may hold values from 0 to 0.2
- resp_keep: float32 [80, 256, 128], P(None, ('grp', 'seq', 'resp')), parts along dimension 1, may hold values from -0.6 to 0
- resp_len: int32 [256], P(('grp', 'seq', 'resp')), parts along dimension 0, may hold values from 32 to 128, as said below
- conv_weight: float32 [4, 5376], replicated, may hold values from -3 to 3
- conv_bias: float32 [5376], replicated, may hold values from -3 to 3
- skip: float32 [80], replicated, may hold values from 0.5 to 1.5
- gain: float32 [5120], replicated, may hold values from 0.25 to 1.75
Outputs:
- prompt_out: bfloat16 [65536, 5120], P(('grp', 'seq', 'resp')), parts along dimension 0
- resp_out: bfloat16 [256, 128, 5120], P(('grp', 'seq', 'resp')), parts along dimension 0
The draws below stay inside these ranges and needn't reach their ends.
There are 8 independent parts, one for each index of `grp`. The reference program is written for one: setup_inputs(seed, part) draws one part's arguments, and reference() takes and returns one part's arrays. A program takes and returns all parts, laid end to end along the dimension named above; an argument that names none is the same for every part. Nothing has to cross between parts.
Inputs may be any that keep to these rules, and one draw needn't show every extreme that they name: `resp_len`: some response fills all 128 positions.
All inputs are finite; a program needn't handle non-finite values.
Results may differ from the reference program's by a relative error of at most 0.0034.
Values may be sent and summed in bfloat16 or wider, within the bound.
No kernel may reach another device: no remote copies, remote signals or barrier semaphores. Data moves between devices by JAX's collectives and lax.ppermute only.
A program may use at most 256 MiB of HBM per device.

```python
import math
import jax
import jax.numpy as jnp
from jax import lax

HEADS = 80
HEAD_DIM = 64
STATE = 128
KERNEL = 4
BLOCK = 128
PT_DEV = 256
RESP_LEN = 128
D_INNER = 5120
CONV_DIM = 5376
PROMPT_TOKENS = 8192
RESPONSES = 32


def head_laws(key):
    seed_key = jax.random.fold_in(key, 9101)
    shuffled = jax.random.permutation(jax.random.fold_in(seed_key, 1), HEADS)
    slow_count = HEADS // 2
    is_slow = shuffled < slow_count
    chain_len = float(PROMPT_TOKENS + RESP_LEN)
    fast_rate = jax.random.uniform(jax.random.fold_in(seed_key, 2), (HEADS,), jnp.float32, 1.0 / 50.0, 1.0 / 30.0)
    slow_rate = jnp.exp(jax.random.uniform(jax.random.fold_in(seed_key, 3), (HEADS,), jnp.float32, math.log(0.2), math.log(0.6))) / chain_len
    head_decay_rate = jnp.where(is_slow, slow_rate, fast_rate)
    step_base = jnp.where(is_slow, 0.2 * math.sqrt(40.0 / chain_len), 0.1)
    return (head_decay_rate, step_base)


def step_roughness(key, shape):
    jaggedness = jnp.exp(jax.random.uniform(key, shape, jnp.float32, math.log(0.5), math.log(2.0)))
    return jaggedness


def keep_roughness(key, shape):
    jaggedness = jax.random.uniform(key, shape, jnp.float32, 0.5, 1.5)
    return jaggedness


def draw_prompt_step(key, part):
    head_decay_rate, step_base = head_laws(key)
    jaggedness = step_roughness(jax.random.fold_in(key, 21), (HEADS, PROMPT_TOKENS))
    return step_base[:, None] * jaggedness


def draw_resp_step(key, part):
    head_decay_rate, step_base = head_laws(key)
    jaggedness = step_roughness(jax.random.fold_in(key, 22), (HEADS, RESPONSES, RESP_LEN))
    return step_base[:, None, None] * jaggedness


def draw_prompt_keep(key, part):
    head_decay_rate, step_base = head_laws(key)
    block_count = PROMPT_TOKENS // PT_DEV
    device_factor = jnp.exp(jax.random.uniform(jax.random.fold_in(key, 31), (block_count,), jnp.float32, math.log(0.7), math.log(1.4)))
    token_multiplier = jnp.repeat(device_factor, PT_DEV)
    jaggedness = keep_roughness(jax.random.fold_in(key, 32), (HEADS, PROMPT_TOKENS))
    spike_location = jax.random.randint(jax.random.fold_in(key, 33), (2,), 0, PROMPT_TOKENS)
    spike_penalty = jax.random.uniform(jax.random.fold_in(key, 34), (2,), jnp.float32, 0.22, 0.5)
    token_places = jnp.arange(PROMPT_TOKENS)
    spike_events = jnp.where(token_places == spike_location[0], spike_penalty[0], 0.0) + jnp.where(token_places == spike_location[1], spike_penalty[1], 0.0)
    return -(head_decay_rate[:, None] * token_multiplier[None, :] * jaggedness) - spike_events[None, :]


def draw_resp_keep(key, part):
    head_decay_rate, step_base = head_laws(key)
    jaggedness = keep_roughness(jax.random.fold_in(key, 35), (HEADS, RESPONSES, RESP_LEN))
    return -(head_decay_rate[:, None, None] * jaggedness)


def draw_resp_len(key, part):
    lengths = jax.random.randint(jax.random.fold_in(key, 41), (RESPONSES,), RESP_LEN // 4, RESP_LEN + 1)
    shuffled = jax.random.permutation(jax.random.fold_in(key, 42), RESPONSES)
    lengths = jnp.where(shuffled == 0, RESP_LEN, lengths)
    lengths = jnp.where(shuffled == 1, RESP_LEN // 4, lengths)
    return lengths.astype(jnp.int32)


def level_of(key, extent, split, low, top_value):
    factor_of, own = 1.0, jax.random.fold_in(key, 6)
    for axis_at, blocks in split:
        steps = jnp.exp(jax.random.uniform(jax.random.fold_in(own, axis_at), (blocks,), jnp.float32, low / len(split), top_value / len(split)))
        factor_of = factor_of * jnp.repeat(steps, extent[axis_at] // blocks).reshape([-1 if axis == axis_at else 1 for axis in range(len(extent))])
    return factor_of


def scatter_about(rng, extent, scale, limit, shards=(), kind=jnp.bfloat16):
    values = scale * jax.random.normal(rng, extent, jnp.float32)
    if shards:
        values = values * level_of(rng, extent, shards, -0.22, 0.18)
    return jnp.clip(values, -limit, limit).astype(kind)


def setup_inputs(seed: int = 0, part: int = 0) -> dict:
    streams_of = jax.random.split(jax.random.key(seed), 14)
    own_keys = jax.random.split(jax.random.fold_in(streams_of[13], part), 14)
    prompt_xbc = scatter_about(own_keys[0], (PROMPT_TOKENS, CONV_DIM), 1.0, 6.0, ((0, 32),))
    prompt_z = scatter_about(own_keys[1], (PROMPT_TOKENS, D_INNER), 1.0, 6.0, ((0, 32),))
    prompt_step = draw_prompt_step(jax.random.fold_in(jax.random.fold_in(streams_of[13], part), 71), part)
    prompt_keep = draw_prompt_keep(jax.random.fold_in(jax.random.fold_in(streams_of[13], part), 71), part)
    resp_xbc = scatter_about(own_keys[4], (RESPONSES, RESP_LEN, CONV_DIM), 1.0, 6.0, ((0, 32),))
    resp_z = scatter_about(own_keys[5], (RESPONSES, RESP_LEN, D_INNER), 1.0, 6.0, ((0, 32),))
    resp_step = draw_resp_step(jax.random.fold_in(jax.random.fold_in(streams_of[13], part), 71), part)
    resp_keep = draw_resp_keep(jax.random.fold_in(jax.random.fold_in(streams_of[13], part), 71), part)
    resp_len = draw_resp_len(jax.random.fold_in(jax.random.fold_in(streams_of[13], part), 71), part)
    conv_weight = scatter_about(streams_of[9], (KERNEL, CONV_DIM), KERNEL ** -0.5, 3.0, (), jnp.float32)
    conv_bias = scatter_about(streams_of[10], (CONV_DIM,), 0.5, 3.0, (), jnp.float32)
    skip = jnp.clip(jax.random.uniform(streams_of[11], (HEADS,), jnp.float32, 0.5, 1.5), 0.5, 1.5)
    gain = jnp.clip(1.0 + 0.15 * jax.random.normal(streams_of[12], (D_INNER,), jnp.float32), 0.25, 1.75)
    return dict(prompt_xbc=prompt_xbc, prompt_z=prompt_z, prompt_step=prompt_step, prompt_keep=prompt_keep, resp_xbc=resp_xbc, resp_z=resp_z, resp_step=resp_step, resp_keep=resp_keep, resp_len=resp_len, conv_weight=conv_weight, conv_bias=conv_bias, skip=skip, gain=gain)


EPS = 1e-05

def conv_silu(input_rows, history, conv_weight, conv_bias):
    row_count = input_rows.shape[0]
    padded = jnp.concatenate([history, input_rows], axis=0).astype(jnp.float32)
    conv_total = jnp.broadcast_to(conv_bias[None, :], (row_count, conv_bias.shape[0]))
    for offset in range(KERNEL):
        conv_total = conv_total + conv_weight[offset][None, :] * padded[offset:offset + row_count]
    return jax.nn.silu(conv_total).astype(jnp.bfloat16)

def block_terms(activations, step_rows, keep_rows, carry_state):
    row_count = activations.shape[0]
    values = activations[:, :D_INNER].reshape(row_count, HEADS, HEAD_DIM)
    key_rows = activations[:, D_INNER:D_INNER + STATE]
    queries = activations[:, D_INNER + STATE:]
    log_cum = jnp.cumsum(keep_rows, axis=1)
    scores = jnp.dot(queries, key_rows.T, preferred_element_type=jnp.float32)
    token_places = jnp.arange(row_count)
    causal = token_places[:, None] >= token_places[None, :]
    log_gap = jnp.where(causal[None], log_cum[:, :, None] - log_cum[:, None, :], -1e+30)
    mixing = (jnp.exp(log_gap) * scores[None] * step_rows[:, None, :]).astype(jnp.bfloat16)
    within = jnp.einsum('hts,shp->thp', mixing.astype(jnp.float32), values.astype(jnp.float32))
    carried_part = jnp.einsum('tn,hpn->thp', queries.astype(jnp.float32), carry_state, precision=lax.Precision.HIGHEST)
    within = within + carried_part * jnp.exp(log_cum).T[:, :, None]
    tail_weight = jnp.exp(log_cum[:, -1:] - log_cum) * step_rows
    weighted = (values.astype(jnp.float32) * tail_weight.T[:, :, None]).astype(jnp.bfloat16)
    added_state = jnp.einsum('thp,tn->hpn', weighted.astype(jnp.float32), key_rows.astype(jnp.float32))
    next_state = jnp.exp(log_cum[:, -1])[:, None, None] * carry_state + added_state
    return (within, next_state)

def run_blocks(activations, step_rows, keep_rows, carry_state, block):
    block_count = activations.shape[0] // block
    act_blocks = activations.reshape(block_count, block, CONV_DIM)
    step_blocks = jnp.transpose(step_rows.reshape(HEADS, block_count, block), (1, 0, 2))
    keep_blocks = jnp.transpose(keep_rows.reshape(HEADS, block_count, block), (1, 0, 2))

    def advance(state_now, pieces):
        within, next_state = block_terms(pieces[0], pieces[1], pieces[2], state_now)
        return (next_state, within)
    final_state, outputs = lax.scan(advance, carry_state, (act_blocks, step_blocks, keep_blocks))
    return (outputs.reshape(block_count * block, HEADS, HEAD_DIM), final_state)

def finish(pre_norm, activations, gate_rows, skip, gain):
    row_count = pre_norm.shape[0]
    values = activations[:, :D_INNER].astype(jnp.float32).reshape(row_count, HEADS, HEAD_DIM)
    mixed_sum = (pre_norm + skip[None, :, None] * values).reshape(row_count, D_INNER)
    gated_rows = mixed_sum * jax.nn.silu(gate_rows.astype(jnp.float32))
    inv_rms = lax.rsqrt(lax.optimization_barrier(jnp.mean(gated_rows * gated_rows, axis=1, keepdims=True)) + EPS)
    return (gated_rows * inv_rms * gain[None, :]).astype(jnp.bfloat16)

def reference(prompt_xbc, prompt_z, prompt_step, prompt_keep, resp_xbc, resp_z, resp_step, resp_keep, resp_len, conv_weight, conv_bias, skip, gain):
    history = jnp.zeros((KERNEL - 1, CONV_DIM), jnp.bfloat16)
    prompt_acts = conv_silu(prompt_xbc, history, conv_weight, conv_bias)
    zero_state = jnp.zeros((HEADS, HEAD_DIM, STATE), jnp.float32)
    pre_norm, final_state = run_blocks(prompt_acts, prompt_step, prompt_keep, zero_state, BLOCK)
    prompt_out = finish(pre_norm, prompt_acts, prompt_z, skip, gain)
    last_rows = prompt_xbc[PROMPT_TOKENS - (KERNEL - 1):]
    response_block = min(BLOCK, RESP_LEN)
    token_places = jnp.arange(RESP_LEN)

    def respond(pieces):
        input_rows, gate_rows, step_rows, keep_rows, length = pieces
        activations = conv_silu(input_rows, last_rows, conv_weight, conv_bias)
        pre_resp, unused = run_blocks(activations, step_rows, keep_rows, final_state, response_block)
        finished = finish(pre_resp, activations, gate_rows, skip, gain)
        return jnp.where((token_places < length)[:, None], finished, jnp.zeros_like(finished))
    resp_out = lax.map(respond, (resp_xbc, resp_z, jnp.transpose(resp_step, (1, 0, 2)), jnp.transpose(resp_keep, (1, 0, 2)), resp_len))
    return (prompt_out, resp_out)
```

```python
import functools

import jax
import jax.numpy as jnp
from jax import lax
from jax.experimental import pallas as pl
from jax.experimental.pallas import tpu as pltpu
from jax.sharding import PartitionSpec as P

HEADS = 80
HEAD_DIM = 64
STATE = 128
KERNEL = 4
BLOCK = 128
D_INNER = 5120
SLABS = 8
SLAB = D_INNER // SLABS
SLAB_HEADS = HEADS // SLABS
PAIRS = SLAB // 128
EXTRA = 16
HIST = 8
HALF_TAIL = (D_INNER + 2 * STATE) // 2
PIECES = -(-HALF_TAIL // SLAB)
EPS = 1e-05
GROUP = ("seq", "resp")
SIDE = 4

F32 = jnp.float32
BF16 = jnp.bfloat16


SMEM = pl.BlockSpec(memory_space=pltpu.SMEM)
VMEM = pl.BlockSpec(memory_space=pltpu.VMEM)


def ordered(kernel, inputs, extra):
    def body(*refs):
        kernel(*refs[:inputs], *refs[inputs + extra :])

    return body


def params(mib=12):
    return pltpu.CompilerParams(vmem_limit_bytes=mib * 2**20)


def whole(kernel, where, arrays, shapes, name, after=(), scratch=(), cost=None):
    return pl.pallas_call(
        ordered(kernel, 1 + len(arrays), len(after)),
        in_specs=[SMEM] + [VMEM] * (len(arrays) + len(after)),
        out_specs=[VMEM] * len(shapes),
        out_shape=[jax.ShapeDtypeStruct(shape, dtype) for shape, dtype in shapes],
        scratch_shapes=list(scratch),
        compiler_params=params(),
        name=name,
    )(where, *arrays, *after)


def silu(value):
    return 0.5 * value * (1.0 + jnp.tanh(0.5 * value))


def spread(table, pair):
    lane = lax.broadcasted_iota(jnp.int32, table.shape, 1)
    return jnp.take_along_axis(table, 2 * pair + lane // HEAD_DIM, axis=1, mode="promise_in_bounds")


def lanes(slab, count=SLAB):
    return pl.ds(pl.multiple_of(slab * SLAB, 128), count)


def first_part(shape):
    return lax.broadcasted_iota(jnp.int32, shape, 1) % HEAD_DIM < HEAD_DIM // 2


def extra_rows(decay, tail):
    wide = jnp.broadcast_to(decay, tail.shape)
    high = wide.astype(BF16).astype(F32)
    coded = jnp.where(first_part(tail.shape), high, wide - high)
    return jnp.where(lax.broadcasted_iota(jnp.int32, tail.shape, 0) == 0, coded, tail).astype(BF16)


def decay_of(rows):
    wide = rows.astype(F32)
    half = HEAD_DIM // 2
    other = jnp.where(first_part(wide.shape), pltpu.roll(wide, SLAB - half, 1), pltpu.roll(wide, half, 1))
    return (wide + other)[0:1]


def tail_rows(rows_ref, half):
    block = jnp.zeros((EXTRA, SLAB), F32)
    place = lax.broadcasted_iota(jnp.int32, block.shape, 0)
    for piece in range(PIECES):
        width = min(SLAB, HALF_TAIL - piece * SLAB)
        start = pl.multiple_of(half * HALF_TAIL + piece * SLAB, 128)
        wide = rows_ref[:, pl.ds(start, width)].astype(F32)
        if width < SLAB:
            wide = jnp.concatenate([wide, jnp.zeros((HIST, SLAB - width), F32)], axis=1)
        for row in range(KERNEL - 1):
            line = wide[HIST - (KERNEL - 1) + row : HIST - (KERNEL - 1) + row + 1]
            block = jnp.where(place == 1 + PIECES * row + piece, line, block)
    return block


def block_table(keep, step):
    lane = lax.broadcasted_iota(jnp.int32, (HEADS, BLOCK), 1)
    cum = keep
    for by in (1, 2, 4, 8, 16, 32, 64):
        cum = cum + jnp.where(lane >= by, pltpu.roll(cum, by, 1), 0.0)
    gap = cum - 0.5 * cum[:, BLOCK - 1 : BLOCK]
    col = jnp.exp(-gap) * step
    blank = jnp.zeros((128 - HEADS, BLOCK), F32)
    return col, jnp.concatenate([jnp.exp(gap), blank], axis=0).T, jnp.concatenate([col, blank], axis=0).T


def tables_kernel(where_ref, keep_ref, step_ref, skip_ref, col_ref, rowt_ref, colt_ref, hcol_ref):
    place = lax.broadcasted_iota(jnp.int32, (8, 128), 0)
    stack = jnp.zeros((8, 128), F32)
    for block in range(2):
        here = slice(block * BLOCK, (block + 1) * BLOCK)
        col_ref[block], rowt, colt_ref[block] = block_table(keep_ref[:, here], step_ref[:, here])
        rowt_ref[block] = rowt
        stack = jnp.where(place == block, rowt[BLOCK - 1 : BLOCK], stack)
    stack = jnp.where(place == 3, jnp.concatenate([skip_ref[...], jnp.zeros((1, 128 - HEADS), F32)], axis=1), stack)
    for pair in range(HEADS // 2):
        at = (pair % PAIRS) * 128
        hcol_ref[pair // PAIRS, :, at : at + 128] = spread(stack, pair)


def conv_columns(rows, hist, weight, bias):
    wide = jnp.concatenate([hist, rows.astype(F32)], axis=0)
    total = bias + weight[KERNEL - 1 : KERNEL] * wide
    for back in range(1, KERNEL):
        total = total + weight[KERNEL - 1 - back : KERNEL - back] * pltpu.roll(wide, back, 0)
    return silu(total[HIST:]).astype(BF16)


def states_kernel(
    where_ref, x_ref, hist_ref, w_ref, b_ref, rows_ref, colt_ref, hcol_ref,
    acts_ref, kq_ref, high_ref, msg_ref, own_ref, weighted_ref, keyt_ref,
):
    core = where_ref[2]
    keep_history = where_ref[3].astype(F32)

    def conv(cols):
        hist = hist_ref[:, cols].astype(F32) * keep_history
        return conv_columns(x_ref[:, cols], hist, w_ref[:, cols], b_ref[:, cols])

    key = conv(slice(D_INNER, D_INNER + STATE))
    kq_ref[:, 0:STATE] = key
    kq_ref[:, STATE : 2 * STATE] = conv(slice(D_INNER + STATE, D_INNER + 2 * STATE))
    keyt_ref[...] = key.astype(F32).T.astype(BF16)

    def slab_states(slab, put):
        shift = lax.rem(128 - SLAB_HEADS * slab, 128)
        colts = [pltpu.roll(colt_ref[block], shift, 1) for block in range(2)]
        for pair in range(PAIRS):
            cols = slice(pair * 128, pair * 128 + 128)
            acts = conv(pl.ds(pl.multiple_of(slab * SLAB + pair * 128, 128), 128))
            acts_ref[slab, :, cols] = acts
            for block in range(2):
                here = slice(block * BLOCK, (block + 1) * BLOCK)
                weight = spread(colts[block], pair) * hcol_ref[slab, block : block + 1, cols]
                weighted_ref[here, cols] = (acts[here].astype(F32) * weight).astype(BF16)
        first = jnp.dot(keyt_ref[:, 0:BLOCK], weighted_ref[0:BLOCK], preferred_element_type=F32)
        second = jnp.dot(keyt_ref[:, BLOCK:], weighted_ref[BLOCK:], preferred_element_type=F32)
        high_ref[slab] = first.astype(BF16)
        put(hcol_ref[slab, 1:2] ** 2 * first + second)

    def sent(at, carry):
        slab = (1 - core) * 4 + at

        def put(state):
            msg_ref[at, 0:STATE] = state.astype(BF16)

        slab_states(slab, put)
        decay = (hcol_ref[slab, 0:1] * hcol_ref[slab, 1:2]) ** 2
        msg_ref[at, STATE:] = extra_rows(decay, jnp.zeros((EXTRA, SLAB), F32))
        return carry

    def kept(at, carry):
        def put(state):
            own_ref[at] = state

        slab_states(core * 4 + at, put)
        return carry

    lax.fori_loop(0, 4, sent, 0)
    slab = (1 - core) * 4
    decay = (hcol_ref[slab, 0:1] * hcol_ref[slab, 1:2]) ** 2
    msg_ref[0, STATE:] = extra_rows(decay, tail_rows(rows_ref, 1 - core))
    lax.fori_loop(0, 4, kept, 0)


def masked_scores(key_query):
    scores = lax.dot_general(
        key_query[:, STATE:], key_query[:, :STATE], (((1,), (1,)), ((), ())), preferred_element_type=F32
    )
    row = lax.broadcasted_iota(jnp.int32, (BLOCK, BLOCK), 0)
    col = lax.broadcasted_iota(jnp.int32, (BLOCK, BLOCK), 1)
    return jnp.where(row >= col, scores, 0.0)


def within_pair(scores, col_rows, values):
    mixes = [(scores * row).astype(BF16) for row in col_rows]
    first = lax.broadcasted_iota(jnp.int32, (BLOCK, 128), 1) < HEAD_DIM
    wide = values.astype(F32)
    stacked = jnp.concatenate(
        [jnp.where(first, wide, 0.0).astype(BF16), jnp.where(first, 0.0, wide).astype(BF16)], axis=0
    )
    return jnp.dot(jnp.concatenate(mixes, axis=1), stacked, preferred_element_type=F32)


def prompt_within_kernel(
    where_ref, acts_ref, z_ref, kq_ref, high_ref, col_ref, rowt_ref, hcol_ref, part_ref, gate_ref, scores_ref
):
    for block in range(2):
        scores_ref[block] = masked_scores(kq_ref[block * BLOCK : (block + 1) * BLOCK, :])

    def step(slab, carry):
        shift = lax.rem(128 - SLAB_HEADS * slab, 128)
        rowts = [pltpu.roll(rowt_ref[block], shift, 1) for block in range(2)]
        earlier = jnp.dot(kq_ref[BLOCK : 2 * BLOCK, STATE:], high_ref[slab], preferred_element_type=F32)
        for pair in range(PAIRS):
            cols = slice(pair * 128, pair * 128 + 128)
            gate_cols = pl.ds(pl.multiple_of(slab * SLAB + pair * 128, 128), 128)
            first_half = hcol_ref[slab, 0:1, cols]
            second_half = hcol_ref[slab, 1:2, cols]
            skip = hcol_ref[slab, 3:4, cols]
            head = slab * SLAB_HEADS + 2 * pair
            for block in range(2):
                here = slice(block * BLOCK, (block + 1) * BLOCK)
                values = acts_ref[slab, here, cols]
                col_rows = [col_ref[block, pl.ds(head + which, 1), :] for which in range(2)]
                mixed = within_pair(scores_ref[block], col_rows, values)
                scale = first_half
                if block == 1:
                    mixed += second_half * earlier[:, cols]
                    scale = second_half * first_half * first_half
                gate = silu(z_ref[here, gate_cols].astype(F32))
                row = spread(rowts[block], pair)
                part_ref[slab, here, cols] = (row * mixed + skip * values.astype(F32)) * gate
                gate_ref[slab, here, cols] = row * scale * gate
        return carry

    lax.fori_loop(0, SLABS, step, 0)


def resp_within_kernel(
    where_ref, x_ref, mine_ref, other_ref, w_ref, b_ref, z_ref, keep_ref, step_ref, hcol_ref,
    part_ref, gate_ref, kq_ref, hist_ref, scores_ref, col_ref, rowt_ref,
):
    core = where_ref[2]
    for half in range(2):
        flag = (core == half).astype(F32)
        tail = mine_ref[...].astype(F32) * flag + other_ref[...].astype(F32) * (1.0 - flag)
        for piece in range(PIECES):
            width = min(SLAB, HALF_TAIL - piece * SLAB)
            start = half * HALF_TAIL + piece * SLAB
            block = jnp.zeros((HIST, SLAB), F32)
            place = lax.broadcasted_iota(jnp.int32, block.shape, 0)
            for row in range(KERNEL - 1):
                at = 1 + PIECES * row + piece
                block = jnp.where(place == HIST - (KERNEL - 1) + row, tail[at : at + 1], block)
            hist_ref[:, start : start + width] = block[:, 0:width]
    col_ref[...], rowt_ref[...], _ = block_table(keep_ref[...], step_ref[...])

    def conv(cols):
        return conv_columns(x_ref[:, cols], hist_ref[:, cols], w_ref[:, cols], b_ref[:, cols])

    for at in (0, STATE):
        kq_ref[:, at : at + STATE] = conv(slice(D_INNER + at, D_INNER + at + STATE))
    scores_ref[...] = masked_scores(kq_ref[...])

    def step(slab, carry):
        rowt = pltpu.roll(rowt_ref[...], lax.rem(128 - SLAB_HEADS * slab, 128), 1)
        for pair in range(PAIRS):
            cols = slice(pair * 128, pair * 128 + 128)
            wide_cols = pl.ds(pl.multiple_of(slab * SLAB + pair * 128, 128), 128)
            values = conv(wide_cols)
            head = slab * SLAB_HEADS + 2 * pair
            col_rows = [col_ref[pl.ds(head + which, 1), :] for which in range(2)]
            mixed = within_pair(scores_ref[...], col_rows, values)
            gate = silu(z_ref[:, wide_cols].astype(F32))
            row = spread(rowt, pair)
            half = row[BLOCK - 1 : BLOCK]
            part_ref[slab, :, cols] = (row * mixed + hcol_ref[slab, 3:4, cols] * values.astype(F32)) * gate
            gate_ref[slab, :, cols] = row * half * gate
        return carry

    lax.fori_loop(0, SLABS, step, 0)


def at_shift(place, by):
    return lax.rem(place + by + SIDE, SIDE)


def pick(condition, value):
    flag = condition.astype(F32)
    return value * flag + (1.0 - flag)


def chip_kernel(where_ref, own_ref, recv_ref, hcol_ref, rows_ref, *out_refs):
    x, core = where_ref[0], where_ref[2]
    first = (core == 0).astype(F32)
    tail = tail_rows(rows_ref, core) * (1.0 - first) + recv_ref[0, STATE:, :].astype(F32) * first
    for shift in range(SIDE):
        slab = at_shift(x, shift)
        half = hcol_ref[core * 4 + slab]
        mine = (half[0:1] * half[1:2]) ** 2
        theirs = decay_of(recv_ref[slab, STATE:, :])
        own_scale = theirs * first + (1.0 - first)
        recv_scale = mine * (1.0 - first) + first
        state = own_scale * own_ref[slab] + recv_scale * recv_ref[slab, 0:STATE, :].astype(F32)
        out_refs[shift][0:STATE] = state.astype(BF16)
        out_refs[shift][STATE:] = extra_rows(mine * theirs, tail)


def row_kernel(where_ref, r0, r1, r2, r3, out_ref):
    x = where_ref[0]
    refs = (r0, r1, r2, r3)
    places = [at_shift(x, -i) for i in range(SIDE)]
    decays = [decay_of(ref[STATE:]) for ref in refs]
    total = jnp.zeros((STATE, SLAB), F32)
    through = jnp.ones((1, SLAB), F32)
    tail = jnp.zeros((EXTRA, SLAB), F32)
    for i in range(SIDE):
        scale = jnp.ones((1, SLAB), F32)
        for k in range(SIDE):
            if k != i:
                scale = scale * pick(places[k] > places[i], decays[k])
        total = total + scale * refs[i][0:STATE].astype(F32)
        through = through * decays[i]
        tail = tail + refs[i][STATE:].astype(F32) * (places[i] == SIDE - 1).astype(F32)
    out_ref[0:STATE] = total.astype(BF16)
    out_ref[STATE:] = extra_rows(through, tail)


def entering_kernel(where_ref, r0, r1, r2, r3, t0, t1, t2, t3, e0, e1, e2, e3, tail_ref):
    x, y = where_ref[0], where_ref[1]
    refs, totals, outs = (r0, r1, r2, r3), (t0, t1, t2, t3), (e0, e1, e2, e3)
    rows = [at_shift(y, -i) for i in range(SIDE)]
    row_decays = [decay_of(ref[STATE:]) for ref in totals]
    final = jnp.zeros((STATE, SLAB), F32)
    row_in = jnp.zeros((STATE, SLAB), F32)
    tail = jnp.zeros((EXTRA, SLAB), F32)
    for i in range(SIDE):
        scale = jnp.ones((1, SLAB), F32)
        before = (rows[i] < y).astype(F32) * jnp.ones((1, SLAB), F32)
        for k in range(SIDE):
            if k != i:
                scale = scale * pick(rows[k] > rows[i], row_decays[k])
                before = before * pick(jnp.logical_and(rows[k] > rows[i], rows[k] < y), row_decays[k])
        wide = totals[i][0:STATE].astype(F32)
        final = final + scale * wide
        row_in = row_in + before * wide
        tail = tail + totals[i][STATE:].astype(F32) * (rows[i] == SIDE - 1).astype(F32)
    tail_ref[...] = tail.astype(BF16)
    final = final.astype(BF16)
    places = [at_shift(x, -i) for i in range(SIDE)]
    decays = [decay_of(ref[STATE:]) for ref in refs]
    for shift in range(SIDE):
        target = at_shift(x, shift)
        carry = jnp.ones((1, SLAB), F32)
        for k in range(SIDE):
            carry = carry * pick(places[k] < target, decays[k])
        total = carry * row_in
        for i in range(SIDE):
            scale = (places[i] < target).astype(F32) * jnp.ones((1, SLAB), F32)
            for k in range(SIDE):
                if k != i:
                    scale = scale * pick(
                        jnp.logical_and(places[k] > places[i], places[k] < target), decays[k]
                    )
            total = total + scale * refs[i][0:STATE].astype(F32)
        outs[shift][0:STATE] = total.astype(BF16)
        outs[shift][STATE:] = final


def cores_kernel(where_ref, g0, g1, g2, g3, own_ref, recv_ref, hcol_ref, mine_ref, send_ref, final_ref):
    x, core = where_ref[0], where_ref[2]
    first = (core == 0).astype(F32)
    for i, ref in enumerate((g0, g1, g2, g3)):
        slab = at_shift(x, -i)
        half = hcol_ref[core * 4 + slab]
        mine = (half[0:1] * half[1:2]) ** 2
        theirs = decay_of(recv_ref[slab, STATE:, :])
        decay = mine * first + theirs * (1.0 - first)
        earlier = own_ref[slab] * first + recv_ref[slab, 0:STATE, :].astype(F32) * (1.0 - first)
        start = ref[0:STATE].astype(F32)
        later = decay * start + earlier
        mine_ref[slab] = (start * first + later * (1.0 - first)).astype(BF16)
        send_ref[slab] = (later * first + start * (1.0 - first)).astype(BF16)
        final_ref[slab] = ref[STATE:]


def finish_kernel(tile, length_at, where_ref, part_ref, gate_ref, kq_ref, mine_ref, other_ref, gain_ref, out_ref, gated_ref):
    core = where_ref[2]
    start = pl.program_id(0) * tile
    here = pl.ds(pl.multiple_of(start, tile), tile)
    query = kq_ref[here, STATE:]
    squares = jnp.zeros((tile, 128), F32)
    for held_ref, half in ((mine_ref, core), (other_ref, 1 - core)):
        for s in range(4):
            slab = half * 4 + s
            carried = jnp.dot(query, held_ref[s], preferred_element_type=F32)
            gated = part_ref[slab, here, :] + gate_ref[slab, here, :] * carried
            gated_ref[slab] = gated
            square = gated * gated
            for pair in range(PAIRS):
                squares = squares + square[:, pair * 128 : pair * 128 + 128]
    mean = jnp.sum(squares, axis=1, keepdims=True) * (1.0 / D_INNER)
    row = lax.broadcasted_iota(jnp.int32, (tile, 1), 0) + start
    inv = jnp.where(row < where_ref[length_at], lax.rsqrt(mean + EPS), 0.0)
    for slab in range(SLABS):
        cols = slice(slab * SLAB, (slab + 1) * SLAB)
        out_ref[:, cols] = (gated_ref[slab] * inv * gain_ref[:, cols]).astype(BF16)


def finish(where, part, gate, kq, mine, other, gain, length_at, name, tile=64):
    rows = part.shape[1]
    return pl.pallas_call(
        functools.partial(finish_kernel, tile, length_at),
        grid=(rows // tile,),
        in_specs=[SMEM] + [VMEM] * 6,
        out_specs=pl.BlockSpec((tile, D_INNER), lambda i: (i, 0)),
        scratch_shapes=[pltpu.VMEM((SLABS, tile, SLAB), F32)],
        out_shape=jax.ShapeDtypeStruct((rows, D_INNER), BF16),
        compiler_params=params(),
        name=name,
    )(where, part, gate, kq, mine, other, gain)


def number(y, x, core):
    return (y % SIDE) * 2 * SIDE + (x % SIDE) * 2 + core


def moved(value, move):
    pairs = [
        (number(y, x, core), number(*move(y, x, core)))
        for y in range(SIDE)
        for x in range(SIDE)
        for core in range(2)
    ]
    return lax.ppermute(value, GROUP, pairs)


def swap_cores(value):
    return moved(value, lambda y, x, core: (y, x, 1 - core))


def along_x(value, by):
    return moved(value, lambda y, x, core: (y, x + by, core))


def along_y(value, by):
    return moved(value, lambda y, x, core: (y + by, x, core))


def make_tables(where, keep, step, skip, after):
    shapes = [((2, HEADS, BLOCK), F32), ((2, BLOCK, 128), F32), ((2, BLOCK, 128), F32), ((SLABS, 8, SLAB), F32)]
    return whole(tables_kernel, where, (keep, step, skip[None, :]), shapes, "tables", after)


def make_states(where, xbc, hist, weight, bias, own_rows, colt, hcol):
    rows = xbc.shape[0]
    shapes = [
        ((SLABS, rows, SLAB), BF16),
        ((rows, 2 * STATE), BF16),
        ((SLABS, STATE, SLAB), BF16),
        ((4, STATE + EXTRA, SLAB), BF16),
        ((4, STATE, SLAB), F32),
    ]
    scratch = [pltpu.VMEM((rows, SLAB), BF16), pltpu.VMEM((STATE, rows), BF16)]
    return whole(states_kernel, where, (xbc, hist, weight, bias, own_rows, colt, hcol), shapes, "states", scratch=scratch)


def prompt_within(where, acts, z, kq, high, col, rowt, hcol, after):
    shapes = [((SLABS, z.shape[0], SLAB), F32)] * 2
    scratch = [pltpu.VMEM((2, BLOCK, BLOCK), F32)]
    return whole(prompt_within_kernel, where, (acts, z, kq, high, col, rowt, hcol), shapes, "prompt_within", after, scratch)


def resp_within(where, xbc, mine, other, weight, bias, z, keep, step, hcol, after):
    rows = z.shape[0]
    shapes = [((SLABS, rows, SLAB), F32)] * 2 + [((rows, 2 * STATE), BF16)]
    scratch = [
        pltpu.VMEM((HIST, D_INNER + 2 * STATE), F32),
        pltpu.VMEM((BLOCK, BLOCK), F32),
        pltpu.VMEM((HEADS, BLOCK), F32),
        pltpu.VMEM((BLOCK, 128), F32),
    ]
    arrays = (xbc, mine, other, weight, bias, z, keep, step, hcol)
    return whole(resp_within_kernel, where, arrays, shapes, "resp_within", after, scratch)


def shards(
    prompt_xbc,
    prompt_z,
    prompt_step,
    prompt_keep,
    resp_xbc,
    resp_z,
    resp_step,
    resp_keep,
    resp_len,
    conv_weight,
    conv_bias,
    skip,
    gain,
):
    rows = prompt_xbc.shape[0]
    seq, core = lax.axis_index("seq"), lax.axis_index("resp")
    fixed = [seq % SIDE, seq // SIDE, core, jnp.where(lax.axis_index(GROUP) == 0, 0, 1)]
    where = jnp.stack([jnp.asarray(v, jnp.int32) for v in fixed + [rows, resp_len[0]]])
    bias_row, gain_row = conv_bias[None, :], gain[None, :]

    own_rows = prompt_xbc[rows - HIST :]
    count = 2 * SIDE * SIDE
    hist = lax.ppermute(own_rows, GROUP, [(i, i + 1) for i in range(count - 1)])
    col, rowt, colt, hcol = make_tables(
        where, prompt_keep, prompt_step, skip, after=(prompt_xbc, conv_weight, bias_row)
    )
    acts, kq, high, msg, own = make_states(where, prompt_xbc, hist, conv_weight, bias_row, own_rows, colt, hcol)
    recv = swap_cores(msg)
    with_extra, both = ((STATE + EXTRA, SLAB), BF16), ((2 * STATE, SLAB), BF16)
    c0, c1, c2, c3 = whole(chip_kernel, where, (own, recv, hcol, own_rows), [with_extra] * 4, "chip")
    pieces = (c0, along_x(c1, 1), along_x(c2, 2), along_x(c3, 3))
    part, gate = prompt_within(where, acts, prompt_z, kq, high, col, rowt, hcol, after=(c1, c2, c3))
    (total,) = whole(row_kernel, where, pieces, [with_extra], "row", after=(part, gate))
    totals = (total, along_y(total, 1), along_y(total, 2), along_y(total, 3))
    e0, e1, e2, e3, tail = whole(
        entering_kernel, where, pieces + totals, [both] * 4 + [((EXTRA, SLAB), BF16)], "entering", after=(part, gate)
    )
    tail_other = swap_cores(tail)
    back = (e0, along_x(e1, 1), along_x(e2, 2), along_x(e3, 3))
    resp_part, resp_gate, resp_kq = resp_within(
        where, resp_xbc[0], tail, tail_other, conv_weight, bias_row, resp_z[0],
        resp_keep.reshape(HEADS, BLOCK), resp_step.reshape(HEADS, BLOCK), hcol, after=(e1, e2, e3),
    )
    four = ((4, STATE, SLAB), BF16)
    mine, send, final = whole(
        cores_kernel, where, back + (own, recv, hcol), [four] * 3, "cores",
        after=(resp_part, resp_gate, part, gate),
    )
    other, final_other = swap_cores(send), swap_cores(final)
    prompt_out = finish(where, part, gate, kq, mine, other, gain_row, 4, "prompt_finish")
    resp_out = finish(where, resp_part, resp_gate, resp_kq, final, final_other, gain_row, 5, "resp_finish")
    return (prompt_out, resp_out[None])


def solution(mesh):
    return jax.shard_map(
        shards,
        mesh=mesh,
        in_specs=(
            P(("grp", "seq", "resp"), None),
            P(("grp", "seq", "resp"), None),
            P(None, ("grp", "seq", "resp")),
            P(None, ("grp", "seq", "resp")),
            P(("grp", "seq", "resp"), None, None),
            P(("grp", "seq", "resp"), None, None),
            P(None, ("grp", "seq", "resp"), None),
            P(None, ("grp", "seq", "resp"), None),
            P(("grp", "seq", "resp")),
            P(),
            P(),
            P(),
            P(),
        ),
        out_specs=(P(("grp", "seq", "resp"), None), P(("grp", "seq", "resp"), None, None)),
        check_vma=False,
    )
```

```python
import functools

import jax
import jax.numpy as jnp
from jax import lax
from jax.experimental import pallas as pl
from jax.experimental.pallas import tpu as pltpu
from jax.sharding import PartitionSpec as P

HEADS = 80
HEAD_DIM = 64
STATE = 128
KERNEL = 4
BLOCK = 128
D_INNER = 5120
SLABS = 8
SLAB = D_INNER // SLABS
SLAB_HEADS = HEADS // SLABS
PAIRS = SLAB // 128
EXTRA = 16
HIST = 8
HALF_TAIL = (D_INNER + 2 * STATE) // 2
PIECES = -(-HALF_TAIL // SLAB)
EPS = 1e-05
GROUP = ("seq", "resp")
SIDE = 4

F32 = jnp.float32
BF16 = jnp.bfloat16


SMEM = pl.BlockSpec(memory_space=pltpu.SMEM)
VMEM = pl.BlockSpec(memory_space=pltpu.VMEM)
HBM = pl.BlockSpec(memory_space=pltpu.HBM)


def ordered(kernel, inputs, extra):
    def body(*refs):
        kernel(*refs[:inputs], *refs[inputs + extra :])

    return body


def params(mib=12):
    return pltpu.CompilerParams(vmem_limit_bytes=mib * 2**20)


def whole(kernel, where, arrays, shapes, name, after=(), scratch=(), outside=0):
    return pl.pallas_call(
        ordered(kernel, 1 + len(arrays), len(after)),
        in_specs=[SMEM] + [HBM] * outside + [VMEM] * (len(arrays) - outside + len(after)),
        out_specs=[VMEM] * len(shapes),
        out_shape=[jax.ShapeDtypeStruct(shape, dtype) for shape, dtype in shapes],
        scratch_shapes=list(scratch),
        compiler_params=params(),
        name=name,
    )(where, *(pltpu.with_memory_space_constraint(a, pltpu.HBM) for a in arrays[:outside]), *arrays[outside:], *after)


def silu(value):
    return 0.5 * value * (1.0 + jnp.tanh(0.5 * value))


def spread(table, pair):
    lane = lax.broadcasted_iota(jnp.int32, table.shape, 1)
    return jnp.take_along_axis(table, 2 * pair + lane // HEAD_DIM, axis=1, mode="promise_in_bounds")


def lanes(slab, count=SLAB):
    return pl.ds(pl.multiple_of(slab * SLAB, 128), count)


def first_part(shape):
    return lax.broadcasted_iota(jnp.int32, shape, 1) % HEAD_DIM < HEAD_DIM // 2


def extra_rows(decay, tail):
    wide = jnp.broadcast_to(decay, tail.shape)
    high = wide.astype(BF16).astype(F32)
    coded = jnp.where(first_part(tail.shape), high, wide - high)
    return jnp.where(lax.broadcasted_iota(jnp.int32, tail.shape, 0) == 0, coded, tail).astype(BF16)


def decay_of(rows):
    wide = rows.astype(F32)
    half = HEAD_DIM // 2
    other = jnp.where(first_part(wide.shape), pltpu.roll(wide, SLAB - half, 1), pltpu.roll(wide, half, 1))
    return (wide + other)[0:1]


def tail_rows(rows_ref, half):
    block = jnp.zeros((EXTRA, SLAB), F32)
    place = lax.broadcasted_iota(jnp.int32, block.shape, 0)
    for piece in range(PIECES):
        width = min(SLAB, HALF_TAIL - piece * SLAB)
        start = pl.multiple_of(half * HALF_TAIL + piece * SLAB, 128)
        wide = rows_ref[:, pl.ds(start, width)].astype(F32)
        if width < SLAB:
            wide = jnp.concatenate([wide, jnp.zeros((HIST, SLAB - width), F32)], axis=1)
        for row in range(KERNEL - 1):
            line = wide[HIST - (KERNEL - 1) + row : HIST - (KERNEL - 1) + row + 1]
            block = jnp.where(place == 1 + PIECES * row + piece, line, block)
    return block


def block_table(keep, step):
    lane = lax.broadcasted_iota(jnp.int32, (HEADS, BLOCK), 1)
    cum = keep
    for by in (1, 2, 4, 8, 16, 32, 64):
        cum = cum + jnp.where(lane >= by, pltpu.roll(cum, by, 1), 0.0)
    gap = cum - 0.5 * cum[:, BLOCK - 1 : BLOCK]
    col = jnp.exp(-gap) * step
    blank = jnp.zeros((128 - HEADS, BLOCK), F32)
    return col, jnp.concatenate([jnp.exp(gap), blank], axis=0).T, jnp.concatenate([col, blank], axis=0).T


def tables_kernel(
    where_ref, keep_from, step_from, skip_ref, col_ref, rowt_ref, colt_ref, hcol_ref, keep_ref, step_ref, sems
):
    copies = [
        pltpu.make_async_copy(keep_from, keep_ref, sems.at[0]),
        pltpu.make_async_copy(step_from, step_ref, sems.at[1]),
    ]
    for copy in copies:
        copy.start()
    for copy in copies:
        copy.wait()
    place = lax.broadcasted_iota(jnp.int32, (8, 128), 0)
    stack = jnp.zeros((8, 128), F32)
    for block in range(2):
        here = slice(block * BLOCK, (block + 1) * BLOCK)
        col_ref[block], rowt, colt_ref[block] = block_table(keep_ref[:, here], step_ref[:, here])
        rowt_ref[block] = rowt
        stack = jnp.where(place == block, rowt[BLOCK - 1 : BLOCK], stack)
    stack = jnp.where(place == 3, jnp.concatenate([skip_ref[...], jnp.zeros((1, 128 - HEADS), F32)], axis=1), stack)
    for pair in range(HEADS // 2):
        at = (pair % PAIRS) * 128
        hcol_ref[pair // PAIRS, :, at : at + 128] = spread(stack, pair)


def conv_columns(rows, hist, weight, bias):
    wide = jnp.concatenate([hist, rows.astype(F32)], axis=0)
    total = bias + weight[KERNEL - 1 : KERNEL] * wide
    for back in range(1, KERNEL):
        total = total + weight[KERNEL - 1 - back : KERNEL - back] * pltpu.roll(wide, back, 0)
    return silu(total[HIST:]).astype(BF16)


def add_states(slab, at, conv, colt_ref, hcol_ref, keyt_ref, acts_ref, high_ref, weighted_ref, put):
    shift = lax.rem(128 - SLAB_HEADS * slab, 128)
    colts = [pltpu.roll(colt_ref[block], shift, 1) for block in range(2)]
    for pair in range(PAIRS):
        cols = slice(pair * 128, pair * 128 + 128)
        acts = conv(pl.ds(pl.multiple_of(slab * SLAB + pair * 128, 128), 128))
        acts_ref[at, :, cols] = acts
        for block in range(2):
            here = slice(block * BLOCK, (block + 1) * BLOCK)
            weight = spread(colts[block], pair) * hcol_ref[slab, block : block + 1, cols]
            weighted_ref[here, cols] = (acts[here].astype(F32) * weight).astype(BF16)
    first = jnp.dot(keyt_ref[:, 0:BLOCK], weighted_ref[0:BLOCK], preferred_element_type=F32)
    second = jnp.dot(keyt_ref[:, BLOCK:], weighted_ref[BLOCK:], preferred_element_type=F32)
    high_ref[at] = first.astype(BF16)
    put(hcol_ref[slab, 1:2] ** 2 * first + second)


def convolver(where_ref, x_ref, hist_ref, w_ref, b_ref):
    keep_history = where_ref[3].astype(F32)

    def conv(cols):
        hist = hist_ref[:, cols].astype(F32) * keep_history
        return conv_columns(x_ref[:, cols], hist, w_ref[:, cols], b_ref[:, cols])

    return conv


def sent_states_kernel(
    where_ref, x_from, w_from, hist_ref, b_ref, rows_ref, colt_ref, hcol_ref,
    acts_ref, kq_ref, keyt_ref, high_ref, msg_ref, x_ref, w_ref, weighted_ref, sems,
):
    half = 1 - where_ref[2]
    kq_cols = pl.ds(D_INNER, 2 * STATE)
    copies = [
        pltpu.make_async_copy(w_from, w_ref, sems.at[0]),
        pltpu.make_async_copy(x_from.at[:, kq_cols], x_ref.at[:, kq_cols], sems.at[1]),
    ]
    for at in range(4):
        cols = pl.ds(pl.multiple_of((half * 4 + at) * SLAB, 128), SLAB)
        copies.append(pltpu.make_async_copy(x_from.at[:, cols], x_ref.at[:, cols], sems.at[2 + at]))
    for copy in copies:
        copy.start()
    conv = convolver(where_ref, x_ref, hist_ref, w_ref, b_ref)
    for copy in copies[:2]:
        copy.wait()
    key = conv(slice(D_INNER, D_INNER + STATE))
    kq_ref[:, 0:STATE] = key
    kq_ref[:, STATE : 2 * STATE] = conv(slice(D_INNER + STATE, D_INNER + 2 * STATE))
    keyt_ref[...] = key.astype(F32).T.astype(BF16)
    for copy in copies[2:]:
        copy.wait()

    def body(at, carry):
        slab = half * 4 + at

        def put(state):
            msg_ref[at, 0:STATE] = state.astype(BF16)

        add_states(slab, at, conv, colt_ref, hcol_ref, keyt_ref, acts_ref, high_ref, weighted_ref, put)
        decay = (hcol_ref[slab, 0:1] * hcol_ref[slab, 1:2]) ** 2
        msg_ref[at, STATE:] = extra_rows(decay, jnp.zeros((EXTRA, SLAB), F32))
        return carry

    lax.fori_loop(0, 4, body, 0)
    slab = half * 4
    decay = (hcol_ref[slab, 0:1] * hcol_ref[slab, 1:2]) ** 2
    msg_ref[0, STATE:] = extra_rows(decay, tail_rows(rows_ref, half))


def kept_states_kernel(
    where_ref, x_ref, w_ref, hist_ref, b_ref, keyt_ref, colt_ref, hcol_ref, acts_ref, high_ref, own_ref, weighted_ref
):
    half = where_ref[2]
    conv = convolver(where_ref, x_ref, hist_ref, w_ref, b_ref)

    def body(at, carry):
        def put(state):
            own_ref[at] = state

        add_states(half * 4 + at, at, conv, colt_ref, hcol_ref, keyt_ref, acts_ref, high_ref, weighted_ref, put)
        return carry

    lax.fori_loop(0, 4, body, 0)


def masked_scores(key_query):
    scores = lax.dot_general(
        key_query[:, STATE:], key_query[:, :STATE], (((1,), (1,)), ((), ())), preferred_element_type=F32
    )
    row = lax.broadcasted_iota(jnp.int32, (BLOCK, BLOCK), 0)
    col = lax.broadcasted_iota(jnp.int32, (BLOCK, BLOCK), 1)
    return jnp.where(row >= col, scores, 0.0)


def within_pair(scores, col_rows, values):
    mixes = [(scores * row).astype(BF16) for row in col_rows]
    first = lax.broadcasted_iota(jnp.int32, (BLOCK, 128), 1) < HEAD_DIM
    wide = values.astype(F32)
    stacked = jnp.concatenate(
        [jnp.where(first, wide, 0.0).astype(BF16), jnp.where(first, 0.0, wide).astype(BF16)], axis=0
    )
    return jnp.dot(jnp.concatenate(mixes, axis=1), stacked, preferred_element_type=F32)


def prompt_within_kernel(
    where_ref, sent_acts, kept_acts, z_ref, kq_ref, sent_high, kept_high, col_ref, rowt_ref, hcol_ref,
    part_ref, gate_ref, scores_ref,
):
    for block in range(2):
        scores_ref[block] = masked_scores(kq_ref[block * BLOCK : (block + 1) * BLOCK, :])

    def step(half, acts_ref, high_ref, at, carry):
        slab = half * 4 + at
        shift = lax.rem(128 - SLAB_HEADS * slab, 128)
        rowts = [pltpu.roll(rowt_ref[block], shift, 1) for block in range(2)]
        earlier = jnp.dot(kq_ref[BLOCK : 2 * BLOCK, STATE:], high_ref[at], preferred_element_type=F32)
        for pair in range(PAIRS):
            cols = slice(pair * 128, pair * 128 + 128)
            gate_cols = pl.ds(pl.multiple_of(slab * SLAB + pair * 128, 128), 128)
            first_half = hcol_ref[slab, 0:1, cols]
            second_half = hcol_ref[slab, 1:2, cols]
            skip = hcol_ref[slab, 3:4, cols]
            head = slab * SLAB_HEADS + 2 * pair
            for block in range(2):
                here = slice(block * BLOCK, (block + 1) * BLOCK)
                values = acts_ref[at, here, cols]
                col_rows = [col_ref[block, pl.ds(head + which, 1), :] for which in range(2)]
                mixed = within_pair(scores_ref[block], col_rows, values)
                scale = first_half
                if block == 1:
                    mixed += second_half * earlier[:, cols]
                    scale = second_half * first_half * first_half
                gate = silu(z_ref[here, gate_cols].astype(F32))
                row = spread(rowts[block], pair)
                part_ref[slab, here, cols] = (row * mixed + skip * values.astype(F32)) * gate
                gate_ref[slab, here, cols] = row * scale * gate
        return carry

    core = where_ref[2]
    lax.fori_loop(0, 4, functools.partial(step, 1 - core, sent_acts, sent_high), 0)
    lax.fori_loop(0, 4, functools.partial(step, core, kept_acts, kept_high), 0)


def resp_within_kernel(
    where_ref, x_ref, mine_ref, other_ref, w_ref, b_ref, z_ref, keep_ref, step_ref, hcol_ref, final_ref,
    part_ref, gate_ref, kq_ref, passed_ref, hist_ref, scores_ref, col_ref, rowt_ref,
):
    core = where_ref[2]
    passed_ref[...] = final_ref[...]
    for half in range(2):
        flag = (core == half).astype(F32)
        tail = mine_ref[...].astype(F32) * flag + other_ref[...].astype(F32) * (1.0 - flag)
        for piece in range(PIECES):
            width = min(SLAB, HALF_TAIL - piece * SLAB)
            start = half * HALF_TAIL + piece * SLAB
            block = jnp.zeros((HIST, SLAB), F32)
            place = lax.broadcasted_iota(jnp.int32, block.shape, 0)
            for row in range(KERNEL - 1):
                at = 1 + PIECES * row + piece
                block = jnp.where(place == HIST - (KERNEL - 1) + row, tail[at : at + 1], block)
            hist_ref[:, start : start + width] = block[:, 0:width]
    col_ref[...], rowt_ref[...], _ = block_table(keep_ref[...], step_ref[...])

    def conv(cols):
        return conv_columns(x_ref[:, cols], hist_ref[:, cols], w_ref[:, cols], b_ref[:, cols])

    for at in (0, STATE):
        kq_ref[:, at : at + STATE] = conv(slice(D_INNER + at, D_INNER + at + STATE))
    scores_ref[...] = masked_scores(kq_ref[...])

    def step(slab, carry):
        rowt = pltpu.roll(rowt_ref[...], lax.rem(128 - SLAB_HEADS * slab, 128), 1)
        for pair in range(PAIRS):
            cols = slice(pair * 128, pair * 128 + 128)
            wide_cols = pl.ds(pl.multiple_of(slab * SLAB + pair * 128, 128), 128)
            values = conv(wide_cols)
            head = slab * SLAB_HEADS + 2 * pair
            col_rows = [col_ref[pl.ds(head + which, 1), :] for which in range(2)]
            mixed = within_pair(scores_ref[...], col_rows, values)
            gate = silu(z_ref[:, wide_cols].astype(F32))
            row = spread(rowt, pair)
            half = row[BLOCK - 1 : BLOCK]
            part_ref[slab, :, cols] = (row * mixed + hcol_ref[slab, 3:4, cols] * values.astype(F32)) * gate
            gate_ref[slab, :, cols] = row * half * gate
        return carry

    lax.fori_loop(0, SLABS, step, 0)


def at_shift(place, by):
    return lax.rem(place + by + SIDE, SIDE)


def pick(condition, value):
    flag = condition.astype(F32)
    return value * flag + (1.0 - flag)


CHUNKS = [slice(at, at + 128) for at in range(0, SLAB, 128)]


def chip_kernel(where_ref, own_ref, recv_ref, hcol_ref, rows_ref, *out_refs):
    x, core = where_ref[0], where_ref[2]
    first = (core == 0).astype(F32)
    tail = tail_rows(rows_ref, core) * (1.0 - first) + recv_ref[0, STATE:, :].astype(F32) * first
    for shift in range(SIDE):
        slab = at_shift(x, shift)
        half = hcol_ref[core * 4 + slab]
        mine = (half[0:1] * half[1:2]) ** 2
        theirs = decay_of(recv_ref[slab, STATE:, :])
        own_scale = theirs * first + (1.0 - first)
        recv_scale = mine * (1.0 - first) + first
        for cols in CHUNKS:
            received = recv_ref[slab, 0:STATE, cols].astype(F32)
            state = own_scale[:, cols] * own_ref[slab, :, cols] + recv_scale[:, cols] * received
            out_refs[shift][0:STATE, cols] = state.astype(BF16)
        out_refs[shift][STATE:] = extra_rows(mine * theirs, tail)


def weights_to(places, decays, target):
    ones = jnp.ones((1, SLAB), F32)
    weights = []
    for i in range(SIDE):
        scale = (places[i] < target).astype(F32) * ones
        for k in range(SIDE):
            if k != i:
                between = jnp.logical_and(places[k] > places[i], places[k] < target)
                scale = scale * pick(between, decays[k])
        weights.append(scale)
    through = ones
    for k in range(SIDE):
        through = through * pick(places[k] < target, decays[k])
    return weights, through


def weighted_sum(weights, refs, cols):
    return sum(w[:, cols] * ref[0:STATE, cols].astype(F32) for w, ref in zip(weights, refs))


def last_tail(places, refs):
    return sum(ref[STATE:].astype(F32) * (place == SIDE - 1).astype(F32) for place, ref in zip(places, refs))


def row_kernel(where_ref, r0, r1, r2, r3, out_ref):
    refs = (r0, r1, r2, r3)
    places = [at_shift(where_ref[0], -i) for i in range(SIDE)]
    weights, through = weights_to(places, [decay_of(ref[STATE:]) for ref in refs], SIDE)
    for cols in CHUNKS:
        out_ref[0:STATE, cols] = weighted_sum(weights, refs, cols).astype(BF16)
    out_ref[STATE:] = extra_rows(through, last_tail(places, refs))


def entering_kernel(where_ref, r0, r1, r2, r3, t0, t1, t2, t3, e0, e1, e2, e3, final_ref, tail_ref):
    x, y = where_ref[0], where_ref[1]
    refs, totals, outs = (r0, r1, r2, r3), (t0, t1, t2, t3), (e0, e1, e2, e3)
    rows = [at_shift(y, -i) for i in range(SIDE)]
    row_decays = [decay_of(ref[STATE:]) for ref in totals]
    to_end, _ = weights_to(rows, row_decays, SIDE)
    to_row, _ = weights_to(rows, row_decays, y)
    places = [at_shift(x, -i) for i in range(SIDE)]
    decays = [decay_of(ref[STATE:]) for ref in refs]
    to_chips = [weights_to(places, decays, at_shift(x, shift)) for shift in range(SIDE)]
    for cols in CHUNKS:
        final_ref[:, cols] = weighted_sum(to_end, totals, cols).astype(BF16)
        row_in = weighted_sum(to_row, totals, cols)
        for out, (weights, through) in zip(outs, to_chips):
            out[:, cols] = (through[:, cols] * row_in + weighted_sum(weights, refs, cols)).astype(BF16)
    tail_ref[...] = last_tail(rows, totals).astype(BF16)


def cores_kernel(where_ref, g0, g1, g2, g3, own_ref, recv_ref, hcol_ref, mine_ref, send_ref):
    x, core = where_ref[0], where_ref[2]
    first = (core == 0).astype(F32)
    last = 1.0 - first
    for i, ref in enumerate((g0, g1, g2, g3)):
        slab = at_shift(x, -i)
        half = hcol_ref[core * 4 + slab]
        mine = (half[0:1] * half[1:2]) ** 2
        decay = mine * first + decay_of(recv_ref[slab, STATE:, :]) * last
        for cols in CHUNKS:
            earlier = own_ref[slab, :, cols] * first + recv_ref[slab, 0:STATE, cols].astype(F32) * last
            start = ref[:, cols].astype(F32)
            later = decay[:, cols] * start + earlier
            mine_ref[slab, :, cols] = (start * first + later * last).astype(BF16)
            send_ref[slab, :, cols] = (later * first + start * last).astype(BF16)


def gather_kernel(where_ref, f0, f1, f2, f3, out_ref):
    for i, ref in enumerate((f0, f1, f2, f3)):
        out_ref[at_shift(where_ref[0], -i)] = ref[...]


TILE = 64


def half_gated(query, held_ref, half, here, part_ref, gate_ref, put):
    squares = jnp.zeros((TILE, 128), F32)
    for s in range(4):
        carried = jnp.dot(query, held_ref[s], preferred_element_type=F32)
        for cols in CHUNKS:
            gated = part_ref[half * 4 + s, here, cols] + gate_ref[half * 4 + s, here, cols] * carried[:, cols]
            put(s, cols, gated)
            squares = squares + gated * gated
    return squares


def own_half_kernel(where_ref, part_ref, gate_ref, kq_ref, held_ref, gated_ref, squares_ref):
    def body(at, carry):
        here = pl.ds(pl.multiple_of(at * TILE, TILE), TILE)

        def put(s, cols, gated):
            gated_ref[s, here, cols] = gated

        query = kq_ref[here, STATE:]
        squares_ref[here, :] = half_gated(query, held_ref, where_ref[2], here, part_ref, gate_ref, put)
        return carry

    lax.fori_loop(0, part_ref.shape[1] // TILE, body, 0)


def own_half(where, part, gate, kq, held, name, after=()):
    rows = part.shape[1]
    shapes = [((4, rows, SLAB), F32), ((rows, 128), F32)]
    return whole(own_half_kernel, where, (part, gate, kq, held), shapes, name, after)


def finish_kernel(
    length_at, where_ref, part_ref, gate_ref, kq_ref, held_ref, own_ref, squares_ref, gain_ref,
    out_ref, token_ref, gated_ref,
):
    core = where_ref[2]
    start = pl.program_id(0) * TILE
    here = pl.ds(pl.multiple_of(start, TILE), TILE)

    def put(s, cols, gated):
        gated_ref[s, :, cols] = gated

    squares = half_gated(kq_ref[here, STATE:], held_ref, 1 - core, here, part_ref, gate_ref, put)
    squares = squares + squares_ref[here, :]
    mean = jnp.sum(squares, axis=1, keepdims=True) * (1.0 / D_INNER)
    row = lax.broadcasted_iota(jnp.int32, (TILE, 1), 0) + start
    inv = jnp.where(row < where_ref[length_at], lax.rsqrt(mean + EPS), 0.0)
    inv = jnp.broadcast_to(inv, (TILE, 128))
    for s in range(4):
        for half, value_of in (
            (core, lambda cols: own_ref[s, here, cols]),
            (1 - core, lambda cols: gated_ref[s, :, cols]),
        ):
            for cols in CHUNKS:
                wide = pl.ds(pl.multiple_of((half * 4 + s) * SLAB + cols.start, 128), 128)
                out_ref[:, wide] = (value_of(cols) * inv * gain_ref[:, wide]).astype(BF16)
    token_ref[...] = jnp.zeros_like(token_ref)


def finish(where, part, gate, kq, held, own, squares, gain, length_at, name):
    rows = part.shape[1]
    return pl.pallas_call(
        functools.partial(finish_kernel, length_at),
        grid=(rows // TILE,),
        in_specs=[SMEM] + [VMEM] * 7,
        out_specs=[pl.BlockSpec((TILE, D_INNER), lambda i: (i, 0)), pl.BlockSpec((8, 128), lambda i: (0, 0))],
        scratch_shapes=[pltpu.VMEM((4, TILE, SLAB), F32)],
        out_shape=[jax.ShapeDtypeStruct((rows, D_INNER), BF16), jax.ShapeDtypeStruct((8, 128), F32)],
        compiler_params=params(),
        name=name,
    )(where, part, gate, kq, held, own, squares, gain)


def number(y, x, core):
    return (y % SIDE) * 2 * SIDE + (x % SIDE) * 2 + core


def moved(value, move):
    pairs = [
        (number(y, x, core), number(*move(y, x, core)))
        for y in range(SIDE)
        for x in range(SIDE)
        for core in range(2)
    ]
    return lax.ppermute(value, GROUP, pairs)


def swap_cores(value):
    return moved(value, lambda y, x, core: (y, x, 1 - core))


def along_x(value, by):
    return moved(value, lambda y, x, core: (y, x + by, core))


def along_y(value, by):
    return moved(value, lambda y, x, core: (y + by, x, core))


def make_tables(where, keep, step, skip):
    shapes = [((2, HEADS, BLOCK), F32), ((2, BLOCK, 128), F32), ((2, BLOCK, 128), F32), ((SLABS, 8, SLAB), F32)]
    scratch = [pltpu.VMEM(keep.shape, F32), pltpu.VMEM(step.shape, F32), pltpu.SemaphoreType.DMA((2,))]
    return whole(tables_kernel, where, (keep, step, skip[None, :]), shapes, "tables", scratch=scratch, outside=2)


def sent_states(where, xbc, weight, hist, bias, own_rows, colt, hcol):
    rows = xbc.shape[0]
    shapes = [
        ((4, rows, SLAB), BF16),
        ((rows, 2 * STATE), BF16),
        ((STATE, rows), BF16),
        ((4, STATE, SLAB), BF16),
        ((4, STATE + EXTRA, SLAB), BF16),
    ]
    scratch = [
        pltpu.VMEM(xbc.shape, BF16),
        pltpu.VMEM(weight.shape, F32),
        pltpu.VMEM((rows, SLAB), BF16),
        pltpu.SemaphoreType.DMA((6,)),
    ]
    arrays = (xbc, weight, hist, bias, own_rows, colt, hcol)
    return whole(sent_states_kernel, where, arrays, shapes, "sent_states", scratch=scratch, outside=2)


def kept_states(where, xbc, weight, hist, bias, keyt, colt, hcol, after):
    rows = xbc.shape[0]
    shapes = [((4, rows, SLAB), BF16), ((4, STATE, SLAB), BF16), ((4, STATE, SLAB), F32)]
    arrays = (xbc, weight, hist, bias, keyt, colt, hcol)
    return whole(kept_states_kernel, where, arrays, shapes, "kept_states", after, [pltpu.VMEM((rows, SLAB), BF16)])


def prompt_within(where, acts, z, kq, high, col, rowt, hcol, after):
    shapes = [((SLABS, z.shape[0], SLAB), F32)] * 2
    scratch = [pltpu.VMEM((2, BLOCK, BLOCK), F32)]
    arrays = (*acts, z, kq, *high, col, rowt, hcol)
    return whole(prompt_within_kernel, where, arrays, shapes, "prompt_within", after, scratch)


def resp_within(where, xbc, mine, other, weight, bias, z, keep, step, hcol, final, after):
    rows = z.shape[0]
    shapes = [((SLABS, rows, SLAB), F32)] * 2 + [((rows, 2 * STATE), BF16), (final.shape, BF16)]
    scratch = [
        pltpu.VMEM((HIST, D_INNER + 2 * STATE), F32),
        pltpu.VMEM((BLOCK, BLOCK), F32),
        pltpu.VMEM((HEADS, BLOCK), F32),
        pltpu.VMEM((BLOCK, 128), F32),
    ]
    arrays = (xbc, mine, other, weight, bias, z, keep, step, hcol, final)
    return whole(resp_within_kernel, where, arrays, shapes, "resp_within", after, scratch)


def shards(
    prompt_xbc,
    prompt_z,
    prompt_step,
    prompt_keep,
    resp_xbc,
    resp_z,
    resp_step,
    resp_keep,
    resp_len,
    conv_weight,
    conv_bias,
    skip,
    gain,
):
    rows = prompt_xbc.shape[0]
    seq, core = lax.axis_index("seq"), lax.axis_index("resp")
    fixed = [seq % SIDE, seq // SIDE, core, jnp.where(lax.axis_index(GROUP) == 0, 0, 1)]
    where = jnp.stack([jnp.asarray(v, jnp.int32) for v in fixed + [rows, resp_len[0]]])
    bias_row, gain_row = conv_bias[None, :], gain[None, :]

    own_rows = prompt_xbc[rows - HIST :]
    count = 2 * SIDE * SIDE
    hist = lax.ppermute(own_rows, GROUP, [(i, i + 1) for i in range(count - 1)])
    col, rowt, colt, hcol = make_tables(where, prompt_keep, prompt_step, skip)
    sent_acts, kq, keyt, sent_high, msg = sent_states(
        where, prompt_xbc, conv_weight, hist, bias_row, own_rows, colt, hcol
    )
    recv = swap_cores(msg)
    kept_acts, kept_high, own = kept_states(
        where, prompt_xbc, conv_weight, hist, bias_row, keyt, colt, hcol, after=(msg,)
    )
    with_extra, plain = ((STATE + EXTRA, SLAB), BF16), ((STATE, SLAB), BF16)
    c0, c1, c2, c3 = whole(chip_kernel, where, (own, recv, hcol, own_rows), [with_extra] * 4, "chip")
    pieces = (c0, along_x(c1, 1), along_x(c2, 2), along_x(c3, 3))
    part, gate = prompt_within(
        where, (sent_acts, kept_acts), prompt_z, kq, (sent_high, kept_high), col, rowt, hcol, after=(c1, c2, c3)
    )
    (total,) = whole(row_kernel, where, pieces, [with_extra], "row", after=(part, gate))
    totals = (total, along_y(total, 1), along_y(total, 2), along_y(total, 3))
    e0, e1, e2, e3, final, tail = whole(
        entering_kernel, where, pieces + totals, [plain] * 5 + [((EXTRA, SLAB), BF16)], "entering", after=(part, gate)
    )
    tail_other = swap_cores(tail)
    back = (e0, along_x(e1, 1), along_x(e2, 2), along_x(e3, 3))
    resp_part, resp_gate, resp_kq, final = resp_within(
        where, resp_xbc[0], tail, tail_other, conv_weight, bias_row, resp_z[0],
        resp_keep.reshape(HEADS, BLOCK), resp_step.reshape(HEADS, BLOCK), hcol, final, after=(e1, e2, e3),
    )
    finals = (final, along_x(final, 1), along_x(final, 2), along_x(final, 3))
    four = ((4, STATE, SLAB), BF16)
    mine, send = whole(
        cores_kernel, where, back + (own, recv, hcol), [four] * 2, "cores", after=(resp_part, resp_gate, part, gate)
    )
    other = swap_cores(send)
    gated, squares = own_half(where, part, gate, kq, mine, "prompt_own_half", after=(send,))
    prompt_out, token = finish(where, part, gate, kq, other, gated, squares, gain_row, 4, "prompt_finish")
    (final_mine,) = whole(gather_kernel, where, finals, [four], "gather", after=(token, resp_part, resp_gate))
    final_other = swap_cores(final_mine)
    gated, squares = own_half(where, resp_part, resp_gate, resp_kq, final_mine, "resp_own_half")
    resp_out, _ = finish(
        where, resp_part, resp_gate, resp_kq, final_other, gated, squares, gain_row, 5, "resp_finish"
    )
    return (prompt_out, resp_out[None])


def solution(mesh):
    return jax.shard_map(
        shards,
        mesh=mesh,
        in_specs=(
            P(("grp", "seq", "resp"), None),
            P(("grp", "seq", "resp"), None),
            P(None, ("grp", "seq", "resp")),
            P(None, ("grp", "seq", "resp")),
            P(("grp", "seq", "resp"), None, None),
            P(("grp", "seq", "resp"), None, None),
            P(None, ("grp", "seq", "resp"), None),
            P(None, ("grp", "seq", "resp"), None),
            P(("grp", "seq", "resp")),
            P(),
            P(),
            P(),
            P(),
        ),
        out_specs=(P(("grp", "seq", "resp"), None), P(("grp", "seq", "resp"), None, None)),
        check_vma=False,
    )
```

```python
import functools

import jax
import jax.numpy as jnp
from jax import lax
from jax.experimental import pallas as pl
from jax.experimental.pallas import tpu as pltpu
from jax.sharding import PartitionSpec as P

HEADS = 80
HEAD_DIM = 64
STATE = 128
KERNEL = 4
BLOCK = 128
D_INNER = 5120
SLABS = 8
SLAB = D_INNER // SLABS
SLAB_HEADS = HEADS // SLABS
PAIRS = SLAB // 128
EXTRA = 16
HIST = 8
HALF_TAIL = (D_INNER + 2 * STATE) // 2
PIECES = -(-HALF_TAIL // SLAB)
EPS = 1e-05
GROUP = ("seq", "resp")
SIDE = 4

F32 = jnp.float32
BF16 = jnp.bfloat16


SMEM = pl.BlockSpec(memory_space=pltpu.SMEM)
VMEM = pl.BlockSpec(memory_space=pltpu.VMEM)
HBM = pl.BlockSpec(memory_space=pltpu.HBM)


def ordered(kernel, inputs, extra):
    def body(*refs):
        kernel(*refs[:inputs], *refs[inputs + extra :])

    return body


def params(mib=12):
    return pltpu.CompilerParams(vmem_limit_bytes=mib * 2**20)


def whole(kernel, where, arrays, shapes, name, after=(), scratch=(), outside=0):
    return pl.pallas_call(
        ordered(kernel, 1 + len(arrays), len(after)),
        in_specs=[SMEM] + [HBM] * outside + [VMEM] * (len(arrays) - outside + len(after)),
        out_specs=[VMEM] * len(shapes),
        out_shape=[jax.ShapeDtypeStruct(shape, dtype) for shape, dtype in shapes],
        scratch_shapes=list(scratch),
        compiler_params=params(),
        cost_estimate=pl.CostEstimate(flops=1, bytes_accessed=1, transcendentals=0),
        name=name,
    )(where, *(pltpu.with_memory_space_constraint(a, pltpu.HBM) for a in arrays[:outside]), *arrays[outside:], *after)


def silu(value):
    return 0.5 * value * (1.0 + jnp.tanh(0.5 * value))


def spread(table, pair):
    lane = lax.broadcasted_iota(jnp.int32, table.shape, 1)
    return jnp.take_along_axis(table, 2 * pair + lane // HEAD_DIM, axis=1, mode="promise_in_bounds")


def row_of_heads(ref, shift):
    row = jnp.concatenate([ref[...], jnp.zeros((1, 128 - HEADS), F32)], axis=1)
    return pltpu.roll(jnp.broadcast_to(row, (8, 128)), shift, 1)


def first_part(shape):
    return lax.broadcasted_iota(jnp.int32, shape, 1) % HEAD_DIM < HEAD_DIM // 2


def extra_rows(decay, tail):
    wide = jnp.broadcast_to(decay, tail.shape)
    high = wide.astype(BF16).astype(F32)
    coded = jnp.where(first_part(tail.shape), high, wide - high)
    return jnp.where(lax.broadcasted_iota(jnp.int32, tail.shape, 0) == 0, coded, tail).astype(BF16)


def decay_of(rows):
    wide = rows.astype(F32)
    half = HEAD_DIM // 2
    other = jnp.where(first_part(wide.shape), pltpu.roll(wide, SLAB - half, 1), pltpu.roll(wide, half, 1))
    return (wide + other)[0:1]


def tail_rows(rows_ref, half):
    block = jnp.zeros((EXTRA, SLAB), F32)
    place = lax.broadcasted_iota(jnp.int32, block.shape, 0)
    for piece in range(PIECES):
        width = min(SLAB, HALF_TAIL - piece * SLAB)
        start = pl.multiple_of(half * HALF_TAIL + piece * SLAB, 128)
        wide = rows_ref[:, pl.ds(start, width)].astype(F32)
        if width < SLAB:
            wide = jnp.concatenate([wide, jnp.zeros((HIST, SLAB - width), F32)], axis=1)
        for row in range(KERNEL - 1):
            line = wide[HIST - (KERNEL - 1) + row : HIST - (KERNEL - 1) + row + 1]
            block = jnp.where(place == 1 + PIECES * row + piece, line, block)
    return block


def block_table(keep, step):
    lane = lax.broadcasted_iota(jnp.int32, (HEADS, BLOCK), 1)
    cum = keep
    for by in (1, 2, 4, 8, 16, 32, 64):
        cum = cum + jnp.where(lane >= by, pltpu.roll(cum, by, 1), 0.0)
    gap = cum - 0.5 * cum[:, BLOCK - 1 : BLOCK]
    col = jnp.exp(-gap) * step
    blank = jnp.zeros((128 - HEADS, BLOCK), F32)
    return col, jnp.concatenate([jnp.exp(gap), blank], axis=0).T, jnp.concatenate([col, blank], axis=0).T


def tables_kernel(
    where_ref, keep_from, step_from, col_ref, rowt_ref, colt_ref, hcol_ref, keep_ref, step_ref, sems
):
    copies = [
        pltpu.make_async_copy(keep_from, keep_ref, sems.at[0]),
        pltpu.make_async_copy(step_from, step_ref, sems.at[1]),
    ]
    for copy in copies:
        copy.start()
    for copy in copies:
        copy.wait()
    place = lax.broadcasted_iota(jnp.int32, (8, 128), 0)
    stack = jnp.zeros((8, 128), F32)
    for block in range(2):
        here = slice(block * BLOCK, (block + 1) * BLOCK)
        col_ref[block], rowt, colt_ref[block] = block_table(keep_ref[:, here], step_ref[:, here])
        rowt_ref[block] = rowt
        stack = jnp.where(place == block, rowt[BLOCK - 1 : BLOCK], stack)
    for pair in range(HEADS // 2):
        at = (pair % PAIRS) * 128
        hcol_ref[pair // PAIRS, :, at : at + 128] = spread(stack, pair)


def conv_columns(rows, hist, weight, bias):
    wide = jnp.concatenate([hist, rows.astype(F32)], axis=0)
    total = bias + weight[KERNEL - 1 : KERNEL] * wide
    for back in range(1, KERNEL):
        total = total + weight[KERNEL - 1 - back : KERNEL - back] * pltpu.roll(wide, back, 0)
    return silu(total[HIST:]).astype(BF16)


def add_states(slab, at, conv, colt_ref, hcol_ref, keyt_ref, acts_ref, high_ref, weighted_ref, put):
    shift = lax.rem(128 - SLAB_HEADS * slab, 128)
    colts = [pltpu.roll(colt_ref[block], shift, 1) for block in range(2)]
    for pair in range(PAIRS):
        cols = slice(pair * 128, pair * 128 + 128)
        acts = conv(pl.ds(pl.multiple_of(slab * SLAB + pair * 128, 128), 128))
        acts_ref[at, :, cols] = acts
        for block in range(2):
            here = slice(block * BLOCK, (block + 1) * BLOCK)
            weight = spread(colts[block], pair) * hcol_ref[slab, block : block + 1, cols]
            weighted_ref[here, cols] = (acts[here].astype(F32) * weight).astype(BF16)
    first = jnp.dot(keyt_ref[:, 0:BLOCK], weighted_ref[0:BLOCK], preferred_element_type=F32)
    second = jnp.dot(keyt_ref[:, BLOCK:], weighted_ref[BLOCK:], preferred_element_type=F32)
    high_ref[at] = first.astype(BF16)
    put(hcol_ref[slab, 1:2] ** 2 * first + second)


def convolver(where_ref, x_ref, hist_ref, w_ref, b_ref):
    keep_history = where_ref[3].astype(F32)

    def conv(cols):
        hist = hist_ref[:, cols].astype(F32) * keep_history
        return conv_columns(x_ref[:, cols], hist, w_ref[:, cols], b_ref[:, cols])

    return conv


def sent_states_kernel(
    where_ref, x_from, w_from, hist_ref, b_ref, rows_ref, colt_ref, hcol_ref,
    acts_ref, kq_ref, keyt_ref, high_ref, msg_ref, x_ref, w_ref, weighted_ref, sems,
):
    half = 1 - where_ref[2]
    kq_cols = pl.ds(D_INNER, 2 * STATE)
    copies = [
        pltpu.make_async_copy(w_from, w_ref, sems.at[0]),
        pltpu.make_async_copy(x_from.at[:, kq_cols], x_ref.at[:, kq_cols], sems.at[1]),
    ]
    for at in range(4):
        cols = pl.ds(pl.multiple_of((half * 4 + at) * SLAB, 128), SLAB)
        copies.append(pltpu.make_async_copy(x_from.at[:, cols], x_ref.at[:, cols], sems.at[2 + at]))
    for copy in copies:
        copy.start()
    conv = convolver(where_ref, x_ref, hist_ref, w_ref, b_ref)
    for copy in copies[:2]:
        copy.wait()
    key = conv(slice(D_INNER, D_INNER + STATE))
    kq_ref[:, 0:STATE] = key
    kq_ref[:, STATE : 2 * STATE] = conv(slice(D_INNER + STATE, D_INNER + 2 * STATE))
    keyt_ref[...] = key.astype(F32).T.astype(BF16)

    def body(at, carry):
        slab = half * 4 + at
        cols = pl.ds(pl.multiple_of(slab * SLAB, 128), SLAB)
        pltpu.make_async_copy(x_from.at[:, cols], x_ref.at[:, cols], sems.at[2 + at]).wait()

        def put(state):
            msg_ref[at, 0:STATE] = state.astype(BF16)

        add_states(slab, at, conv, colt_ref, hcol_ref, keyt_ref, acts_ref, high_ref, weighted_ref, put)
        decay = (hcol_ref[slab, 0:1] * hcol_ref[slab, 1:2]) ** 2
        msg_ref[at, STATE:] = extra_rows(decay, jnp.zeros((EXTRA, SLAB), F32))
        return carry

    lax.fori_loop(0, 4, body, 0)
    slab = half * 4
    decay = (hcol_ref[slab, 0:1] * hcol_ref[slab, 1:2]) ** 2
    msg_ref[0, STATE:] = extra_rows(decay, tail_rows(rows_ref, half))


def kept_states_kernel(
    where_ref, x_ref, w_ref, hist_ref, b_ref, keyt_ref, colt_ref, hcol_ref, acts_ref, high_ref, own_ref, weighted_ref
):
    half = where_ref[2]
    conv = convolver(where_ref, x_ref, hist_ref, w_ref, b_ref)

    def body(at, carry):
        def put(state):
            own_ref[at] = state

        add_states(half * 4 + at, at, conv, colt_ref, hcol_ref, keyt_ref, acts_ref, high_ref, weighted_ref, put)
        return carry

    lax.fori_loop(0, 4, body, 0)


def masked_scores(key_query):
    scores = lax.dot_general(
        key_query[:, STATE:], key_query[:, :STATE], (((1,), (1,)), ((), ())), preferred_element_type=F32
    )
    row = lax.broadcasted_iota(jnp.int32, (BLOCK, BLOCK), 0)
    col = lax.broadcasted_iota(jnp.int32, (BLOCK, BLOCK), 1)
    return jnp.where(row >= col, scores, 0.0)


def within_pair(scores, col_rows, values):
    mixes = [(scores * row).astype(BF16) for row in col_rows]
    first = lax.broadcasted_iota(jnp.int32, (BLOCK, 128), 1) < HEAD_DIM
    wide = values.astype(F32)
    stacked = jnp.concatenate(
        [jnp.where(first, wide, 0.0).astype(BF16), jnp.where(first, 0.0, wide).astype(BF16)], axis=0
    )
    return jnp.dot(jnp.concatenate(mixes, axis=1), stacked, preferred_element_type=F32)


def prompt_within_kernel(
    where_ref, sent_acts, kept_acts, z_ref, kq_ref, sent_high, kept_high, col_ref, rowt_ref, hcol_ref, skip_ref,
    part_ref, gate_ref, scores_ref,
):
    for block in range(2):
        scores_ref[block] = masked_scores(kq_ref[block * BLOCK : (block + 1) * BLOCK, :])

    def step(half, acts_ref, high_ref, at, carry):
        slab = half * 4 + at
        shift = lax.rem(128 - SLAB_HEADS * slab, 128)
        rowts = [pltpu.roll(rowt_ref[block], shift, 1) for block in range(2)]
        skips = row_of_heads(skip_ref, shift)
        earlier = jnp.dot(kq_ref[BLOCK : 2 * BLOCK, STATE:], high_ref[at], preferred_element_type=F32)
        for pair in range(PAIRS):
            cols = slice(pair * 128, pair * 128 + 128)
            gate_cols = pl.ds(pl.multiple_of(slab * SLAB + pair * 128, 128), 128)
            first_half = hcol_ref[slab, 0:1, cols]
            second_half = hcol_ref[slab, 1:2, cols]
            skip = spread(skips, pair)[0:1]
            head = slab * SLAB_HEADS + 2 * pair
            for block in range(2):
                here = slice(block * BLOCK, (block + 1) * BLOCK)
                values = acts_ref[at, here, cols]
                col_rows = [col_ref[block, pl.ds(head + which, 1), :] for which in range(2)]
                mixed = within_pair(scores_ref[block], col_rows, values)
                scale = first_half
                if block == 1:
                    mixed += second_half * earlier[:, cols]
                    scale = second_half * first_half * first_half
                gate = silu(z_ref[here, gate_cols].astype(F32))
                row = spread(rowts[block], pair)
                part_ref[slab, here, cols] = (row * mixed + skip * values.astype(F32)) * gate
                gate_ref[slab, here, cols] = row * scale * gate
        return carry

    core = where_ref[2]
    lax.fori_loop(0, 4, functools.partial(step, 1 - core, sent_acts, sent_high), 0)
    lax.fori_loop(0, 4, functools.partial(step, core, kept_acts, kept_high), 0)


def resp_within_kernel(
    where_ref, x_ref, mine_ref, other_ref, w_ref, b_ref, z_ref, keep_ref, step_ref, skip_ref,
    part_ref, gate_ref, kq_ref, hist_ref, scores_ref, col_ref, rowt_ref,
):
    core = where_ref[2]
    for half in range(2):
        flag = (core == half).astype(F32)
        tail = mine_ref[...].astype(F32) * flag + other_ref[...].astype(F32) * (1.0 - flag)
        for piece in range(PIECES):
            width = min(SLAB, HALF_TAIL - piece * SLAB)
            start = half * HALF_TAIL + piece * SLAB
            block = jnp.zeros((HIST, SLAB), F32)
            place = lax.broadcasted_iota(jnp.int32, block.shape, 0)
            for row in range(KERNEL - 1):
                at = 1 + PIECES * row + piece
                block = jnp.where(place == HIST - (KERNEL - 1) + row, tail[at : at + 1], block)
            hist_ref[:, start : start + width] = block[:, 0:width]
    col_ref[...], rowt_ref[...], _ = block_table(keep_ref[...], step_ref[...])

    def conv(cols):
        return conv_columns(x_ref[:, cols], hist_ref[:, cols], w_ref[:, cols], b_ref[:, cols])

    for at in (0, STATE):
        kq_ref[:, at : at + STATE] = conv(slice(D_INNER + at, D_INNER + at + STATE))
    scores_ref[...] = masked_scores(kq_ref[...])

    def step(slab, carry):
        shift = lax.rem(128 - SLAB_HEADS * slab, 128)
        rowt = pltpu.roll(rowt_ref[...], shift, 1)
        skips = row_of_heads(skip_ref, shift)
        for pair in range(PAIRS):
            cols = slice(pair * 128, pair * 128 + 128)
            wide_cols = pl.ds(pl.multiple_of(slab * SLAB + pair * 128, 128), 128)
            values = conv(wide_cols)
            head = slab * SLAB_HEADS + 2 * pair
            col_rows = [col_ref[pl.ds(head + which, 1), :] for which in range(2)]
            mixed = within_pair(scores_ref[...], col_rows, values)
            gate = silu(z_ref[:, wide_cols].astype(F32))
            row = spread(rowt, pair)
            half = row[BLOCK - 1 : BLOCK]
            part_ref[slab, :, cols] = (row * mixed + spread(skips, pair)[0:1] * values.astype(F32)) * gate
            gate_ref[slab, :, cols] = row * half * gate
        return carry

    lax.fori_loop(0, SLABS, step, 0)


def at_shift(place, by):
    return lax.rem(place + by + SIDE, SIDE)


def pick(condition, value):
    flag = condition.astype(F32)
    return value * flag + (1.0 - flag)


CHUNKS = [slice(at, at + 128) for at in range(0, SLAB, 128)]


def chip_kernel(where_ref, own_ref, recv_ref, hcol_ref, rows_ref, *out_refs):
    x, core = where_ref[0], where_ref[2]
    first = (core == 0).astype(F32)
    tail = tail_rows(rows_ref, core) * (1.0 - first) + recv_ref[0, STATE:, :].astype(F32) * first
    for shift in range(SIDE):
        slab = at_shift(x, shift)
        half = hcol_ref[core * 4 + slab]
        mine = (half[0:1] * half[1:2]) ** 2
        theirs = decay_of(recv_ref[slab, STATE:, :])
        own_scale = theirs * first + (1.0 - first)
        recv_scale = mine * (1.0 - first) + first
        for cols in CHUNKS:
            received = recv_ref[slab, 0:STATE, cols].astype(F32)
            state = own_scale[:, cols] * own_ref[slab, :, cols] + recv_scale[:, cols] * received
            out_refs[shift][0:STATE, cols] = state.astype(BF16)
        out_refs[shift][STATE:] = extra_rows(mine * theirs, tail)


def weights_to(places, decays, target):
    ones = jnp.ones((1, SLAB), F32)
    weights = []
    for i in range(SIDE):
        scale = (places[i] < target).astype(F32) * ones
        for k in range(SIDE):
            if k != i:
                between = jnp.logical_and(places[k] > places[i], places[k] < target)
                scale = scale * pick(between, decays[k])
        weights.append(scale)
    through = ones
    for k in range(SIDE):
        through = through * pick(places[k] < target, decays[k])
    return weights, through


def weighted_sum(weights, refs, cols):
    return sum(w[:, cols] * ref[0:STATE, cols].astype(F32) for w, ref in zip(weights, refs))


def last_tail(places, refs):
    return sum(ref[STATE:].astype(F32) * (place == SIDE - 1).astype(F32) for place, ref in zip(places, refs))


def direction(state_ref):
    total = jnp.zeros((STATE, 128), F32)
    for cols in CHUNKS:
        state = state_ref[:, cols]
        total = total + state * jnp.sum(state, axis=0, keepdims=True)
    along = jnp.sum(total, axis=1, keepdims=True)
    along = along * (1.0 / (jnp.max(jnp.abs(along)) + 1e-30))
    along = jnp.broadcast_to(along.astype(BF16).astype(F32), (STATE, 128))
    return along, jnp.sum(along * along, axis=0, keepdims=True) + 1e-30


def split_off(state_ref, along, square, out_ref):
    highs, lows = [], []
    for cols in CHUNKS:
        state = state_ref[:, cols]
        factor = jnp.sum(state * along, axis=0, keepdims=True) / square
        high = factor.astype(BF16).astype(F32)
        low = (factor - high).astype(BF16).astype(F32)
        out_ref[0:STATE, cols] = (state - along * (high + low)).astype(BF16)
        highs.append(high)
        lows.append(low)
    return highs, lows


def as_columns(row):
    return jnp.broadcast_to(row, (STATE, 128)).T


def joined(ref, along, factor, cols):
    return ref[0:STATE, cols].astype(F32) + along * factor[:, cols]


def row_kernel(where_ref, r2, r0, r1, r3, out_ref, state_ref):
    refs = (r0, r1, r2, r3)
    places = [at_shift(where_ref[0], -i) for i in range(SIDE)]
    weights, through = weights_to(places, [decay_of(ref[STATE:]) for ref in refs], SIDE)
    for cols in CHUNKS:
        state_ref[:, cols] = weighted_sum(weights, refs, cols)
    along, square = direction(state_ref)
    highs, lows = split_off(state_ref, along, square, out_ref)
    tail = last_tail(places, refs)
    blank = jnp.zeros((1, 128), F32)
    lines = [
        jnp.concatenate([blank] + highs[:4], axis=1),
        jnp.concatenate([blank] + lows[:4], axis=1),
        jnp.concatenate([blank, highs[4], lows[4], along.T[0:1], blank], axis=1),
    ]
    place = lax.broadcasted_iota(jnp.int32, tail.shape, 0)
    for row, line in enumerate(lines):
        tail = tail + jnp.where(place == PIECES * (row + 1), line, 0.0)
    out_ref[STATE:] = extra_rows(through, tail)


def entering_kernel(where_ref, t2, t0, t1, t3, r2, r0, r1, r3, e0, e1, e2, e3, final_ref, tail_ref, state_ref):
    x, y = where_ref[0], where_ref[1]
    refs, totals, outs = (r0, r1, r2, r3), (t0, t1, t2, t3), (e0, e1, e2, e3)
    rows = [at_shift(y, -i) for i in range(SIDE)]
    row_decays = [decay_of(ref[STATE:]) for ref in totals]
    to_end, _ = weights_to(rows, row_decays, SIDE)
    to_row, _ = weights_to(rows, row_decays, y)
    places = [at_shift(x, -i) for i in range(SIDE)]
    decays = [decay_of(ref[STATE:]) for ref in refs]
    to_chips = [weights_to(places, decays, at_shift(x, shift)) for shift in range(SIDE)]
    coded = []
    for ref in totals:
        wide = ref[STATE:].astype(F32)
        high = jnp.concatenate([wide[PIECES : PIECES + 1, 128:], wide[3 * PIECES : 3 * PIECES + 1, 128:256]], axis=1)
        low = jnp.concatenate(
            [wide[2 * PIECES : 2 * PIECES + 1, 128:], wide[3 * PIECES : 3 * PIECES + 1, 256:384]], axis=1
        )
        coded.append((as_columns(wide[3 * PIECES : 3 * PIECES + 1, 384:512]), high + low))
    for cols in CHUNKS:
        states = [joined(ref, along, factor, cols) for ref, (along, factor) in zip(totals, coded)]
        state_ref[SIDE, :, cols] = sum(w[:, cols] * state for w, state in zip(to_end, states))
        row_in = sum(w[:, cols] * state for w, state in zip(to_row, states))
        for shift, (weights, through) in enumerate(to_chips):
            state_ref[shift, :, cols] = through[:, cols] * row_in + weighted_sum(weights, refs, cols)
    along, square = direction(state_ref.at[SIDE])
    line = jnp.concatenate([along.T[0:1], jnp.zeros((1, SLAB - 128), F32)], axis=1)
    place = lax.broadcasted_iota(jnp.int32, (EXTRA, SLAB), 0)
    for at, out in enumerate(outs + (final_ref,)):
        highs, lows = split_off(state_ref.at[at], along, square, out)
        block = jnp.where(place == 0, jnp.concatenate(highs, axis=1), jnp.where(place == 1, jnp.concatenate(lows, axis=1), 0.0))
        out[STATE:] = jnp.where(place == 2, line, block).astype(BF16)
    tail_ref[...] = last_tail(rows, totals).astype(BF16)


def put_pair(ref, slab, cols, state):
    high = state.astype(BF16)
    ref[slab, 0:STATE, cols] = high
    ref[slab, STATE:, cols] = (state - high.astype(F32)).astype(BF16)


def uncoded(ref):
    wide = ref[STATE:].astype(F32)
    return as_columns(wide[2:3, 0:128]), wide[0:1] + wide[1:2]


def cores_kernel(
    where_ref, g2, g0, g1, g3, f2, f0, f1, f3, own_ref, recv_ref, hcol_ref, mine_ref, send_ref, final_ref
):
    x, core = where_ref[0], where_ref[2]
    first = (core == 0).astype(F32)
    last = 1.0 - first
    for i, (ref, passed_ref) in enumerate(zip((g0, g1, g2, g3), (f0, f1, f2, f3))):
        slab = at_shift(x, -i)
        half = hcol_ref[core * 4 + slab]
        mine = (half[0:1] * half[1:2]) ** 2
        decay = mine * first + decay_of(recv_ref[slab, STATE:, :]) * last
        along, factor = uncoded(ref)
        final_along, final_factor = uncoded(passed_ref)
        for cols in CHUNKS:
            put_pair(final_ref, slab, cols, joined(passed_ref, final_along, final_factor, cols))
            earlier = own_ref[slab, :, cols] * first + recv_ref[slab, 0:STATE, cols].astype(F32) * last
            start = joined(ref, along, factor, cols)
            later = decay[:, cols] * start + earlier
            put_pair(mine_ref, slab, cols, start * first + later * last)
            put_pair(send_ref, slab, cols, later * first + start * last)


TILE = 64


def half_gated(query, held_ref, half, here, part_ref, gate_ref, put):
    squares = jnp.zeros((TILE, 128), F32)
    twice = jnp.concatenate([query, query], axis=1)
    for s in range(4):
        carried = jnp.dot(twice, held_ref[s], preferred_element_type=F32)
        for cols in CHUNKS:
            gated = part_ref[half * 4 + s, here, cols] + gate_ref[half * 4 + s, here, cols] * carried[:, cols]
            put(s, cols, gated)
            squares = squares + gated * gated
    return squares


def own_half_kernel(where_ref, part_ref, gate_ref, kq_ref, held_ref, gated_ref, squares_ref):
    def body(at, carry):
        here = pl.ds(pl.multiple_of(at * TILE, TILE), TILE)

        def put(s, cols, gated):
            gated_ref[s, here, cols] = gated

        query = kq_ref[here, STATE:]
        squares_ref[here, :] = half_gated(query, held_ref, where_ref[2], here, part_ref, gate_ref, put)
        return carry

    lax.fori_loop(0, part_ref.shape[1] // TILE, body, 0)


def own_half(where, part, gate, kq, held, name, after=()):
    rows = part.shape[1]
    shapes = [((4, rows, SLAB), F32), ((rows, 128), F32)]
    return whole(own_half_kernel, where, (part, gate, kq, held), shapes, name, after)


def finish_kernel(
    length_at, where_ref, part_ref, gate_ref, kq_ref, held_ref, own_ref, squares_ref, gain_ref,
    out_ref, token_ref, gated_ref, rows_ref, sems,
):
    core = where_ref[2]

    def copy_out(at):
        here = pl.ds(pl.multiple_of(at * TILE, TILE), TILE)
        return pltpu.make_async_copy(rows_ref.at[here], out_ref.at[here], sems.at[at])

    def body(at, carry):
        start = at * TILE
        here = pl.ds(pl.multiple_of(start, TILE), TILE)

        def put(s, cols, gated):
            gated_ref[s, :, cols] = gated

        squares = half_gated(kq_ref[here, STATE:], held_ref, 1 - core, here, part_ref, gate_ref, put)
        squares = squares + squares_ref[here, :]
        mean = jnp.sum(squares, axis=1, keepdims=True) * (1.0 / D_INNER)
        row = lax.broadcasted_iota(jnp.int32, (TILE, 1), 0) + start
        inv = jnp.where(row < where_ref[length_at], lax.rsqrt(mean + EPS), 0.0)
        inv = jnp.broadcast_to(inv, (TILE, 128))
        for s in range(4):
            for half, value_of in (
                (core, lambda cols: own_ref[s, here, cols]),
                (1 - core, lambda cols: gated_ref[s, :, cols]),
            ):
                for cols in CHUNKS:
                    wide = pl.ds(pl.multiple_of((half * 4 + s) * SLAB + cols.start, 128), 128)
                    rows_ref[here, wide] = (value_of(cols) * inv * gain_ref[:, wide]).astype(BF16)
        copy_out(at).start()
        return carry

    tiles = part_ref.shape[1] // TILE
    lax.fori_loop(0, tiles, body, 0)
    token_ref[...] = jnp.zeros_like(token_ref)
    for at in range(tiles):
        copy_out(at).wait()


def finish(where, part, gate, kq, held, own, squares, gain, length_at, name, after):
    rows = part.shape[1]
    return pl.pallas_call(
        ordered(functools.partial(finish_kernel, length_at), 8, len(after)),
        in_specs=[SMEM] + [VMEM] * (7 + len(after)),
        out_specs=[HBM, VMEM],
        scratch_shapes=[
            pltpu.VMEM((4, TILE, SLAB), F32),
            pltpu.VMEM((rows, D_INNER), BF16),
            pltpu.SemaphoreType.DMA((rows // TILE,)),
        ],
        out_shape=[jax.ShapeDtypeStruct((rows, D_INNER), BF16), jax.ShapeDtypeStruct((8, 128), F32)],
        compiler_params=params(),
        cost_estimate=pl.CostEstimate(flops=1, bytes_accessed=1, transcendentals=0),
        name=name,
    )(where, part, gate, kq, held, own, squares, gain, *after)


def number(y, x, core):
    return (y % SIDE) * 2 * SIDE + (x % SIDE) * 2 + core


def moved(value, move):
    pairs = [
        (number(y, x, core), number(*move(y, x, core)))
        for y in range(SIDE)
        for x in range(SIDE)
        for core in range(2)
    ]
    return lax.ppermute(value, GROUP, pairs)


def swap_cores(value):
    return moved(value, lambda y, x, core: (y, x, 1 - core))


def along_x(value, by):
    return moved(value, lambda y, x, core: (y, x + by, core))


def round_x(here, to_next, to_opposite, to_last):
    opposite = along_x(to_opposite, 2)
    return opposite, here, along_x(to_next, 1), along_x(to_last, 3)


def along_y(value, by):
    return moved(value, lambda y, x, core: (y + by, x, core))


def make_tables(where, keep, step):
    shapes = [((2, HEADS, BLOCK), F32), ((2, BLOCK, 128), F32), ((2, BLOCK, 128), F32), ((SLABS, 8, SLAB), F32)]
    scratch = [pltpu.VMEM(keep.shape, F32), pltpu.VMEM(step.shape, F32), pltpu.SemaphoreType.DMA((2,))]
    return whole(tables_kernel, where, (keep, step), shapes, "tables", scratch=scratch, outside=2)


def sent_states(where, xbc, weight, hist, bias, own_rows, colt, hcol):
    rows = xbc.shape[0]
    shapes = [
        ((4, rows, SLAB), BF16),
        ((rows, 2 * STATE), BF16),
        ((STATE, rows), BF16),
        ((4, STATE, SLAB), BF16),
        ((4, STATE + EXTRA, SLAB), BF16),
    ]
    scratch = [
        pltpu.VMEM(xbc.shape, BF16),
        pltpu.VMEM(weight.shape, F32),
        pltpu.VMEM((rows, SLAB), BF16),
        pltpu.SemaphoreType.DMA((6,)),
    ]
    arrays = (xbc, weight, hist, bias, own_rows, colt, hcol)
    return whole(sent_states_kernel, where, arrays, shapes, "sent_states", scratch=scratch, outside=2)


def kept_states(where, xbc, weight, hist, bias, keyt, colt, hcol, after):
    rows = xbc.shape[0]
    shapes = [((4, rows, SLAB), BF16), ((4, STATE, SLAB), BF16), ((4, STATE, SLAB), F32)]
    arrays = (xbc, weight, hist, bias, keyt, colt, hcol)
    return whole(kept_states_kernel, where, arrays, shapes, "kept_states", after, [pltpu.VMEM((rows, SLAB), BF16)])


def prompt_within(where, acts, z, kq, high, col, rowt, hcol, skip, after):
    shapes = [((SLABS, z.shape[0], SLAB), F32)] * 2
    scratch = [pltpu.VMEM((2, BLOCK, BLOCK), F32)]
    arrays = (*acts, z, kq, *high, col, rowt, hcol, skip)
    return whole(prompt_within_kernel, where, arrays, shapes, "prompt_within", after, scratch)


def resp_within(where, xbc, mine, other, weight, bias, z, keep, step, skip, after):
    rows = z.shape[0]
    shapes = [((SLABS, rows, SLAB), F32)] * 2 + [((rows, 2 * STATE), BF16)]
    scratch = [
        pltpu.VMEM((HIST, D_INNER + 2 * STATE), F32),
        pltpu.VMEM((BLOCK, BLOCK), F32),
        pltpu.VMEM((HEADS, BLOCK), F32),
        pltpu.VMEM((BLOCK, 128), F32),
    ]
    arrays = (xbc, mine, other, weight, bias, z, keep, step, skip)
    return whole(resp_within_kernel, where, arrays, shapes, "resp_within", after, scratch)


def shards(
    prompt_xbc,
    prompt_z,
    prompt_step,
    prompt_keep,
    resp_xbc,
    resp_z,
    resp_step,
    resp_keep,
    resp_len,
    conv_weight,
    conv_bias,
    skip,
    gain,
):
    rows = prompt_xbc.shape[0]
    seq, core = lax.axis_index("seq"), lax.axis_index("resp")
    fixed = [seq % SIDE, seq // SIDE, core, jnp.where(lax.axis_index(GROUP) == 0, 0, 1)]
    where = jnp.stack([jnp.asarray(v, jnp.int32) for v in fixed + [rows, resp_len[0]]])
    bias_row, gain_row, skip_row = conv_bias[None, :], gain[None, :], skip[None, :]

    own_rows = prompt_xbc[rows - HIST :]
    count = 2 * SIDE * SIDE
    hist = lax.ppermute(own_rows, GROUP, [(i, i + 1) for i in range(count - 1)])
    col, rowt, colt, hcol = make_tables(where, prompt_keep, prompt_step)
    sent_acts, kq, keyt, sent_high, msg = sent_states(
        where, prompt_xbc, conv_weight, hist, bias_row, own_rows, colt, hcol
    )
    recv = swap_cores(msg)
    kept_acts, kept_high, own = kept_states(
        where, prompt_xbc, conv_weight, hist, bias_row, keyt, colt, hcol, after=(msg,)
    )
    with_extra = ((STATE + EXTRA, SLAB), BF16)
    c0, c1, c2, c3 = whole(chip_kernel, where, (own, recv, hcol, own_rows), [with_extra] * 4, "chip")
    pieces = round_x(c0, c1, c2, c3)
    part, gate = prompt_within(
        where, (sent_acts, kept_acts), prompt_z, kq, (sent_high, kept_high), col, rowt, hcol, skip_row,
        after=(c1, c2, c3),
    )
    (total,) = whole(row_kernel, where, pieces, [with_extra], "row", after=(part, gate), scratch=[pltpu.VMEM((STATE, SLAB), F32)])
    opposite = along_y(total, 2)
    totals = (opposite, total, along_y(total, 1), along_y(total, 3))
    e0, e1, e2, e3, final, tail = whole(
        entering_kernel, where, totals + pieces, [with_extra] * 5 + [((EXTRA, SLAB), BF16)], "entering", after=(part, gate),
        scratch=[pltpu.VMEM((SIDE + 1, STATE, SLAB), F32)],
    )
    tail_other = swap_cores(tail)
    back = round_x(e0, e1, e2, e3)
    finals = round_x(final, final, final, final)
    resp_part, resp_gate, resp_kq = resp_within(
        where, resp_xbc[0], tail, tail_other, conv_weight, bias_row, resp_z[0],
        resp_keep.reshape(HEADS, BLOCK), resp_step.reshape(HEADS, BLOCK), skip_row, after=(e1, e2, e3),
    )
    four = ((4, 2 * STATE, SLAB), BF16)
    mine, send, final_mine = whole(
        cores_kernel,
        where,
        back + finals + (own, recv, hcol),
        [four] * 3,
        "cores",
        after=(resp_part, resp_gate, part, gate),
    )
    other, final_other = swap_cores(send), swap_cores(final_mine)
    gated, squares = own_half(where, part, gate, kq, mine, "prompt_own_half", after=(send,))
    resp_gated, resp_squares = own_half(
        where, resp_part, resp_gate, resp_kq, final_mine, "resp_own_half", after=(squares,)
    )
    prompt_out, token = finish(
        where, part, gate, kq, other, gated, squares, gain_row, 4, "prompt_finish", after=(resp_squares,)
    )
    resp_out, _ = finish(
        where, resp_part, resp_gate, resp_kq, final_other, resp_gated, resp_squares, gain_row, 5, "resp_finish",
        after=(token,),
    )
    return (prompt_out, resp_out[None])


def solution(mesh):
    return jax.shard_map(
        shards,
        mesh=mesh,
        in_specs=(
            P(("grp", "seq", "resp"), None),
            P(("grp", "seq", "resp"), None),
            P(None, ("grp", "seq", "resp")),
            P(None, ("grp", "seq", "resp")),
            P(("grp", "seq", "resp"), None, None),
            P(("grp", "seq", "resp"), None, None),
            P(None, ("grp", "seq", "resp"), None),
            P(None, ("grp", "seq", "resp"), None),
            P(("grp", "seq", "resp")),
            P(),
            P(),
            P(),
            P(),
        ),
        out_specs=(P(("grp", "seq", "resp"), None), P(("grp", "seq", "resp"), None, None)),
        check_vma=False,
    )
```

```python
import functools

import jax
import jax.numpy as jnp
from jax import lax
from jax.experimental import pallas as pl
from jax.experimental.pallas import tpu as pltpu
from jax.sharding import PartitionSpec as P

HEADS = 80
HEAD_DIM = 64
STATE = 128
KERNEL = 4
BLOCK = 128
D_INNER = 5120
SLABS = 8
SLAB = D_INNER // SLABS
SLAB_HEADS = HEADS // SLABS
PAIRS = SLAB // 128
EXTRA = 16
HIST = 8
HALF_TAIL = (D_INNER + 2 * STATE) // 2
PIECES = -(-HALF_TAIL // SLAB)
EPS = 1e-05
GROUP = ("seq", "resp")
SIDE = 4

F32 = jnp.float32
BF16 = jnp.bfloat16


SMEM = pl.BlockSpec(memory_space=pltpu.SMEM)
VMEM = pl.BlockSpec(memory_space=pltpu.VMEM)
HBM = pl.BlockSpec(memory_space=pltpu.HBM)


def ordered(kernel, inputs, extra):
    def body(*refs):
        kernel(*refs[:inputs], *refs[inputs + extra :])

    return body


def params(mib=12):
    return pltpu.CompilerParams(vmem_limit_bytes=mib * 2**20)


def whole(kernel, where, arrays, shapes, name, after=(), scratch=(), outside=0):
    return pl.pallas_call(
        ordered(kernel, 1 + len(arrays), len(after)),
        in_specs=[SMEM] + [HBM] * outside + [VMEM] * (len(arrays) - outside + len(after)),
        out_specs=[VMEM] * len(shapes),
        out_shape=[jax.ShapeDtypeStruct(shape, dtype) for shape, dtype in shapes],
        scratch_shapes=list(scratch),
        compiler_params=params(),
        cost_estimate=pl.CostEstimate(flops=1, bytes_accessed=1, transcendentals=0),
        name=name,
    )(where, *(pltpu.with_memory_space_constraint(a, pltpu.HBM) for a in arrays[:outside]), *arrays[outside:], *after)


def silu(value):
    return 0.5 * value * (1.0 + jnp.tanh(0.5 * value))


def spread(table, pair):
    lane = lax.broadcasted_iota(jnp.int32, table.shape, 1)
    return jnp.take_along_axis(table, 2 * pair + lane // HEAD_DIM, axis=1, mode="promise_in_bounds")


def row_of_heads(ref, shift):
    row = jnp.concatenate([ref[...], jnp.zeros((1, 128 - HEADS), F32)], axis=1)
    return pltpu.roll(jnp.broadcast_to(row, (8, 128)), shift, 1)


def first_part(shape):
    return lax.broadcasted_iota(jnp.int32, shape, 1) % HEAD_DIM < HEAD_DIM // 2


def extra_rows(decay, tail):
    wide = jnp.broadcast_to(decay, tail.shape)
    high = wide.astype(BF16).astype(F32)
    coded = jnp.where(first_part(tail.shape), high, wide - high)
    return jnp.where(lax.broadcasted_iota(jnp.int32, tail.shape, 0) == 0, coded, tail).astype(BF16)


def decay_of(rows):
    wide = rows.astype(F32)
    half = HEAD_DIM // 2
    other = jnp.where(first_part(wide.shape), pltpu.roll(wide, SLAB - half, 1), pltpu.roll(wide, half, 1))
    return (wide + other)[0:1]


def tail_rows(rows_ref, half):
    block = jnp.zeros((EXTRA, SLAB), F32)
    place = lax.broadcasted_iota(jnp.int32, block.shape, 0)
    for piece in range(PIECES):
        width = min(SLAB, HALF_TAIL - piece * SLAB)
        start = pl.multiple_of(half * HALF_TAIL + piece * SLAB, 128)
        wide = rows_ref[:, pl.ds(start, width)].astype(F32)
        if width < SLAB:
            wide = jnp.concatenate([wide, jnp.zeros((HIST, SLAB - width), F32)], axis=1)
        for row in range(KERNEL - 1):
            line = wide[HIST - (KERNEL - 1) + row : HIST - (KERNEL - 1) + row + 1]
            block = jnp.where(place == 1 + PIECES * row + piece, line, block)
    return block


def block_table(keep, step):
    lane = lax.broadcasted_iota(jnp.int32, (HEADS, BLOCK), 1)
    cum = keep
    for by in (1, 2, 4, 8, 16, 32, 64):
        cum = cum + jnp.where(lane >= by, pltpu.roll(cum, by, 1), 0.0)
    gap = cum - 0.5 * cum[:, BLOCK - 1 : BLOCK]
    col = jnp.exp(-gap) * step
    blank = jnp.zeros((128 - HEADS, BLOCK), F32)
    return col, jnp.concatenate([jnp.exp(gap), blank], axis=0).T, jnp.concatenate([col, blank], axis=0).T


def tables_kernel(
    where_ref, keep_from, step_from, x_from, w_from, col_ref, rowt_ref, colt_ref, hcol_ref, x_ref, w_ref,
    keep_ref, step_ref, sems,
):
    copies = [
        pltpu.make_async_copy(keep_from, keep_ref, sems.at[0]),
        pltpu.make_async_copy(step_from, step_ref, sems.at[1]),
        pltpu.make_async_copy(w_from, w_ref, sems.at[2]),
    ]
    share = x_ref.shape[0] // 4
    for at in range(4):
        rows = pl.ds(at * share, share)
        copies.append(pltpu.make_async_copy(x_from.at[rows], x_ref.at[rows], sems.at[3 + at]))
    for copy in copies:
        copy.start()
    for copy in copies[:2]:
        copy.wait()
    place = lax.broadcasted_iota(jnp.int32, (8, 128), 0)
    stack = jnp.zeros((8, 128), F32)
    for block in range(2):
        here = slice(block * BLOCK, (block + 1) * BLOCK)
        col_ref[block], rowt, colt_ref[block] = block_table(keep_ref[:, here], step_ref[:, here])
        rowt_ref[block] = rowt
        stack = jnp.where(place == block, rowt[BLOCK - 1 : BLOCK], stack)
    for pair in range(HEADS // 2):
        at = (pair % PAIRS) * 128
        hcol_ref[pair // PAIRS, :, at : at + 128] = spread(stack, pair)
    for copy in copies[2:]:
        copy.wait()


def conv_columns(rows, hist, weight, bias):
    wide = jnp.concatenate([hist, rows.astype(F32)], axis=0)
    total = bias + weight[KERNEL - 1 : KERNEL] * wide
    for back in range(1, KERNEL):
        total = total + weight[KERNEL - 1 - back : KERNEL - back] * pltpu.roll(wide, back, 0)
    return silu(total[HIST:]).astype(BF16)


def add_states(slab, at, conv, colt_ref, hcol_ref, keyt_ref, acts_ref, high_ref, weighted_ref, put):
    shift = lax.rem(128 - SLAB_HEADS * slab, 128)
    colts = [pltpu.roll(colt_ref[block], shift, 1) for block in range(2)]
    for pair in range(PAIRS):
        cols = slice(pair * 128, pair * 128 + 128)
        acts = conv(pl.ds(pl.multiple_of(slab * SLAB + pair * 128, 128), 128))
        acts_ref[at, :, cols] = acts
        for block in range(2):
            here = slice(block * BLOCK, (block + 1) * BLOCK)
            weight = spread(colts[block], pair) * hcol_ref[slab, block : block + 1, cols]
            weighted_ref[here, cols] = (acts[here].astype(F32) * weight).astype(BF16)
    first = jnp.dot(keyt_ref[:, 0:BLOCK], weighted_ref[0:BLOCK], preferred_element_type=F32)
    second = jnp.dot(keyt_ref[:, BLOCK:], weighted_ref[BLOCK:], preferred_element_type=F32)
    high_ref[at] = first.astype(BF16)
    put(hcol_ref[slab, 1:2] ** 2 * first + second)


def convolver(where_ref, x_ref, hist_ref, w_ref, b_ref):
    keep_history = where_ref[3].astype(F32)

    def conv(cols):
        hist = hist_ref[:, cols].astype(F32) * keep_history
        return conv_columns(x_ref[:, cols], hist, w_ref[:, cols], b_ref[:, cols])

    return conv


def sent_states_kernel(
    where_ref, x_ref, w_ref, hist_ref, b_ref, rows_ref, colt_ref, hcol_ref,
    acts_ref, kq_ref, keyt_ref, high_ref, msg_ref, weighted_ref,
):
    half = 1 - where_ref[2]
    conv = convolver(where_ref, x_ref, hist_ref, w_ref, b_ref)
    key = conv(slice(D_INNER, D_INNER + STATE))
    kq_ref[:, 0:STATE] = key
    kq_ref[:, STATE : 2 * STATE] = conv(slice(D_INNER + STATE, D_INNER + 2 * STATE))
    keyt_ref[...] = key.astype(F32).T.astype(BF16)

    def body(at, carry):
        slab = half * 4 + at

        def put(state):
            msg_ref[at, 0:STATE] = state.astype(BF16)

        add_states(slab, at, conv, colt_ref, hcol_ref, keyt_ref, acts_ref, high_ref, weighted_ref, put)
        decay = (hcol_ref[slab, 0:1] * hcol_ref[slab, 1:2]) ** 2
        msg_ref[at, STATE:] = extra_rows(decay, jnp.zeros((EXTRA, SLAB), F32))
        return carry

    lax.fori_loop(0, 4, body, 0)
    slab = half * 4
    decay = (hcol_ref[slab, 0:1] * hcol_ref[slab, 1:2]) ** 2
    msg_ref[0, STATE:] = extra_rows(decay, tail_rows(rows_ref, half))


def kept_states_kernel(
    where_ref, x_ref, w_ref, hist_ref, b_ref, keyt_ref, colt_ref, hcol_ref, acts_ref, high_ref, own_ref, weighted_ref
):
    half = where_ref[2]
    conv = convolver(where_ref, x_ref, hist_ref, w_ref, b_ref)

    def body(at, carry):
        def put(state):
            own_ref[at] = state

        add_states(half * 4 + at, at, conv, colt_ref, hcol_ref, keyt_ref, acts_ref, high_ref, weighted_ref, put)
        return carry

    lax.fori_loop(0, 4, body, 0)


def masked_scores(key_query):
    scores = lax.dot_general(
        key_query[:, STATE:], key_query[:, :STATE], (((1,), (1,)), ((), ())), preferred_element_type=F32
    )
    row = lax.broadcasted_iota(jnp.int32, (BLOCK, BLOCK), 0)
    col = lax.broadcasted_iota(jnp.int32, (BLOCK, BLOCK), 1)
    return jnp.where(row >= col, scores, 0.0)


def within_pair(scores, col_rows, values):
    mixes = [(scores * row).astype(BF16) for row in col_rows]
    first = lax.broadcasted_iota(jnp.int32, (BLOCK, 128), 1) < HEAD_DIM
    wide = values.astype(F32)
    stacked = jnp.concatenate(
        [jnp.where(first, wide, 0.0).astype(BF16), jnp.where(first, 0.0, wide).astype(BF16)], axis=0
    )
    return jnp.dot(jnp.concatenate(mixes, axis=1), stacked, preferred_element_type=F32)


def prompt_within_kernel(
    where_ref, sent_acts, kept_acts, z_ref, kq_ref, sent_high, kept_high, col_ref, rowt_ref, hcol_ref, skip_ref,
    part_ref, gate_ref, scores_ref,
):
    for block in range(2):
        scores_ref[block] = masked_scores(kq_ref[block * BLOCK : (block + 1) * BLOCK, :])

    def step(half, acts_ref, high_ref, at, carry):
        slab = half * 4 + at
        shift = lax.rem(128 - SLAB_HEADS * slab, 128)
        rowts = [pltpu.roll(rowt_ref[block], shift, 1) for block in range(2)]
        skips = row_of_heads(skip_ref, shift)
        earlier = jnp.dot(kq_ref[BLOCK : 2 * BLOCK, STATE:], high_ref[at], preferred_element_type=F32)
        for pair in range(PAIRS):
            cols = slice(pair * 128, pair * 128 + 128)
            gate_cols = pl.ds(pl.multiple_of(slab * SLAB + pair * 128, 128), 128)
            first_half = hcol_ref[slab, 0:1, cols]
            second_half = hcol_ref[slab, 1:2, cols]
            skip = spread(skips, pair)[0:1]
            head = slab * SLAB_HEADS + 2 * pair
            for block in range(2):
                here = slice(block * BLOCK, (block + 1) * BLOCK)
                values = acts_ref[at, here, cols]
                col_rows = [col_ref[block, pl.ds(head + which, 1), :] for which in range(2)]
                mixed = within_pair(scores_ref[block], col_rows, values)
                scale = first_half
                if block == 1:
                    mixed += second_half * earlier[:, cols]
                    scale = second_half * first_half * first_half
                gate = silu(z_ref[here, gate_cols].astype(F32))
                row = spread(rowts[block], pair)
                part_ref[slab, here, cols] = (row * mixed + skip * values.astype(F32)) * gate
                gate_ref[slab, here, cols] = row * scale * gate
        return carry

    core = where_ref[2]
    lax.fori_loop(0, 4, functools.partial(step, 1 - core, sent_acts, sent_high), 0)
    lax.fori_loop(0, 4, functools.partial(step, core, kept_acts, kept_high), 0)


def resp_within_kernel(
    where_ref, x_ref, mine_ref, other_ref, w_ref, b_ref, z_ref, keep_ref, step_ref, skip_ref,
    part_ref, gate_ref, kq_ref, hist_ref, scores_ref, col_ref, rowt_ref,
):
    core = where_ref[2]
    for half in range(2):
        flag = (core == half).astype(F32)
        tail = mine_ref[...].astype(F32) * flag + other_ref[...].astype(F32) * (1.0 - flag)
        for piece in range(PIECES):
            width = min(SLAB, HALF_TAIL - piece * SLAB)
            start = half * HALF_TAIL + piece * SLAB
            block = jnp.zeros((HIST, SLAB), F32)
            place = lax.broadcasted_iota(jnp.int32, block.shape, 0)
            for row in range(KERNEL - 1):
                at = 1 + PIECES * row + piece
                block = jnp.where(place == HIST - (KERNEL - 1) + row, tail[at : at + 1], block)
            hist_ref[:, start : start + width] = block[:, 0:width]
    col_ref[...], rowt_ref[...], _ = block_table(keep_ref[...], step_ref[...])

    def conv(cols):
        return conv_columns(x_ref[:, cols], hist_ref[:, cols], w_ref[:, cols], b_ref[:, cols])

    for at in (0, STATE):
        kq_ref[:, at : at + STATE] = conv(slice(D_INNER + at, D_INNER + at + STATE))
    scores_ref[...] = masked_scores(kq_ref[...])

    def step(slab, carry):
        shift = lax.rem(128 - SLAB_HEADS * slab, 128)
        rowt = pltpu.roll(rowt_ref[...], shift, 1)
        skips = row_of_heads(skip_ref, shift)
        for pair in range(PAIRS):
            cols = slice(pair * 128, pair * 128 + 128)
            wide_cols = pl.ds(pl.multiple_of(slab * SLAB + pair * 128, 128), 128)
            values = conv(wide_cols)
            head = slab * SLAB_HEADS + 2 * pair
            col_rows = [col_ref[pl.ds(head + which, 1), :] for which in range(2)]
            mixed = within_pair(scores_ref[...], col_rows, values)
            gate = silu(z_ref[:, wide_cols].astype(F32))
            row = spread(rowt, pair)
            half = row[BLOCK - 1 : BLOCK]
            part_ref[slab, :, cols] = (row * mixed + spread(skips, pair)[0:1] * values.astype(F32)) * gate
            gate_ref[slab, :, cols] = row * half * gate
        return carry

    lax.fori_loop(0, SLABS, step, 0)


def at_shift(place, by):
    return lax.rem(place + by + SIDE, SIDE)


def pick(condition, value):
    flag = condition.astype(F32)
    return value * flag + (1.0 - flag)


CHUNKS = [slice(at, at + 128) for at in range(0, SLAB, 128)]


def chip_kernel(where_ref, own_ref, recv_ref, hcol_ref, rows_ref, *out_refs):
    x, core = where_ref[0], where_ref[2]
    first = (core == 0).astype(F32)
    tail = tail_rows(rows_ref, core) * (1.0 - first) + recv_ref[0, STATE:, :].astype(F32) * first
    for shift in range(SIDE):
        slab = at_shift(x, shift)
        half = hcol_ref[core * 4 + slab]
        mine = (half[0:1] * half[1:2]) ** 2
        theirs = decay_of(recv_ref[slab, STATE:, :])
        own_scale = theirs * first + (1.0 - first)
        recv_scale = mine * (1.0 - first) + first
        for cols in CHUNKS:
            received = recv_ref[slab, 0:STATE, cols].astype(F32)
            state = own_scale[:, cols] * own_ref[slab, :, cols] + recv_scale[:, cols] * received
            out_refs[shift][0:STATE, cols] = state.astype(BF16)
        out_refs[shift][STATE:] = extra_rows(mine * theirs, tail)


def weights_to(places, decays, target):
    ones = jnp.ones((1, SLAB), F32)
    weights = []
    for i in range(SIDE):
        scale = (places[i] < target).astype(F32) * ones
        for k in range(SIDE):
            if k != i:
                between = jnp.logical_and(places[k] > places[i], places[k] < target)
                scale = scale * pick(between, decays[k])
        weights.append(scale)
    through = ones
    for k in range(SIDE):
        through = through * pick(places[k] < target, decays[k])
    return weights, through


def weighted_sum(weights, refs, cols):
    return sum(w[:, cols] * ref[0:STATE, cols].astype(F32) for w, ref in zip(weights, refs))


def last_tail(places, refs):
    return sum(ref[STATE:].astype(F32) * (place == SIDE - 1).astype(F32) for place, ref in zip(places, refs))


def direction(state_ref):
    total = jnp.zeros((STATE, 128), F32)
    for cols in CHUNKS:
        state = state_ref[:, cols]
        total = total + state * jnp.sum(state, axis=0, keepdims=True)
    along = jnp.sum(total, axis=1, keepdims=True)
    along = along * (1.0 / (jnp.max(jnp.abs(along)) + 1e-30))
    along = jnp.broadcast_to(along.astype(BF16).astype(F32), (STATE, 128))
    return along, jnp.sum(along * along, axis=0, keepdims=True) + 1e-30


def split_off(state_ref, along, square, out_ref):
    highs, lows = [], []
    for cols in CHUNKS:
        state = state_ref[:, cols]
        factor = jnp.sum(state * along, axis=0, keepdims=True) / square
        high = factor.astype(BF16).astype(F32)
        low = (factor - high).astype(BF16).astype(F32)
        out_ref[0:STATE, cols] = (state - along * (high + low)).astype(BF16)
        highs.append(high)
        lows.append(low)
    return highs, lows


def as_columns(row):
    return jnp.broadcast_to(row, (STATE, 128)).T


def joined(ref, along, factor, cols):
    return ref[0:STATE, cols].astype(F32) + along * factor[:, cols]


def row_kernel(where_ref, r0, r1, r3, r2, out_ref, state_ref):
    refs = (r0, r1, r2, r3)
    places = [at_shift(where_ref[0], -i) for i in range(SIDE)]
    weights, through = weights_to(places, [decay_of(ref[STATE:]) for ref in refs], SIDE)
    for cols in CHUNKS:
        state_ref[:, cols] = weighted_sum(weights, refs, cols)
    along, square = direction(state_ref)
    highs, lows = split_off(state_ref, along, square, out_ref)
    tail = last_tail(places, refs)
    blank = jnp.zeros((1, 128), F32)
    lines = [
        jnp.concatenate([blank] + highs[:4], axis=1),
        jnp.concatenate([blank] + lows[:4], axis=1),
        jnp.concatenate([blank, highs[4], lows[4], along.T[0:1], blank], axis=1),
    ]
    place = lax.broadcasted_iota(jnp.int32, tail.shape, 0)
    for row, line in enumerate(lines):
        tail = tail + jnp.where(place == PIECES * (row + 1), line, 0.0)
    out_ref[STATE:] = extra_rows(through, tail)


def entering_kernel(where_ref, t0, t1, t3, t2, r0, r1, r3, r2, e0, e1, e2, e3, final_ref, tail_ref, state_ref):
    x, y = where_ref[0], where_ref[1]
    refs, totals, outs = (r0, r1, r2, r3), (t0, t1, t2, t3), (e0, e1, e2, e3)
    rows = [at_shift(y, -i) for i in range(SIDE)]
    row_decays = [decay_of(ref[STATE:]) for ref in totals]
    to_end, _ = weights_to(rows, row_decays, SIDE)
    to_row, _ = weights_to(rows, row_decays, y)
    places = [at_shift(x, -i) for i in range(SIDE)]
    decays = [decay_of(ref[STATE:]) for ref in refs]
    to_chips = [weights_to(places, decays, at_shift(x, shift)) for shift in range(SIDE)]
    coded = []
    for ref in totals:
        wide = ref[STATE:].astype(F32)
        high = jnp.concatenate([wide[PIECES : PIECES + 1, 128:], wide[3 * PIECES : 3 * PIECES + 1, 128:256]], axis=1)
        low = jnp.concatenate(
            [wide[2 * PIECES : 2 * PIECES + 1, 128:], wide[3 * PIECES : 3 * PIECES + 1, 256:384]], axis=1
        )
        coded.append((as_columns(wide[3 * PIECES : 3 * PIECES + 1, 384:512]), high + low))
    for cols in CHUNKS:
        states = [joined(ref, along, factor, cols) for ref, (along, factor) in zip(totals, coded)]
        state_ref[SIDE, :, cols] = sum(w[:, cols] * state for w, state in zip(to_end, states))
        row_in = sum(w[:, cols] * state for w, state in zip(to_row, states))
        for shift, (weights, through) in enumerate(to_chips):
            state_ref[shift, :, cols] = through[:, cols] * row_in + weighted_sum(weights, refs, cols)
    along, square = direction(state_ref.at[SIDE])
    line = jnp.concatenate([along.T[0:1], jnp.zeros((1, SLAB - 128), F32)], axis=1)
    place = lax.broadcasted_iota(jnp.int32, (EXTRA, SLAB), 0)
    for at, out in enumerate(outs + (final_ref,)):
        highs, lows = split_off(state_ref.at[at], along, square, out)
        block = jnp.where(place == 0, jnp.concatenate(highs, axis=1), jnp.where(place == 1, jnp.concatenate(lows, axis=1), 0.0))
        out[STATE:] = jnp.where(place == 2, line, block).astype(BF16)
    tail_ref[...] = last_tail(rows, totals).astype(BF16)


def put_pair(ref, slab, cols, state):
    high = state.astype(BF16)
    ref[slab, 0:STATE, cols] = high
    ref[slab, STATE:, cols] = (state - high.astype(F32)).astype(BF16)


def uncoded(ref):
    wide = ref[STATE:].astype(F32)
    return as_columns(wide[2:3, 0:128]), wide[0:1] + wide[1:2]


def cores_kernel(
    where_ref, g0, g1, g3, g2, f0, f1, f3, f2, own_ref, recv_ref, hcol_ref, mine_ref, send_ref, final_ref
):
    x, core = where_ref[0], where_ref[2]
    first = (core == 0).astype(F32)
    last = 1.0 - first
    for i, (ref, passed_ref) in enumerate(zip((g0, g1, g2, g3), (f0, f1, f2, f3))):
        slab = at_shift(x, -i)
        half = hcol_ref[core * 4 + slab]
        mine = (half[0:1] * half[1:2]) ** 2
        decay = mine * first + decay_of(recv_ref[slab, STATE:, :]) * last
        along, factor = uncoded(ref)
        final_along, final_factor = uncoded(passed_ref)
        for cols in CHUNKS:
            put_pair(final_ref, slab, cols, joined(passed_ref, final_along, final_factor, cols))
            earlier = own_ref[slab, :, cols] * first + recv_ref[slab, 0:STATE, cols].astype(F32) * last
            start = joined(ref, along, factor, cols)
            later = decay[:, cols] * start + earlier
            put_pair(mine_ref, slab, cols, start * first + later * last)
            put_pair(send_ref, slab, cols, later * first + start * last)


TILE = 128
PART = 32


def half_gated(query, held_ref, half, here, part_ref, gate_ref, put):
    squares = jnp.zeros((TILE, 128), F32)
    twice = jnp.concatenate([query, query], axis=1)
    for s in range(4):
        carried = jnp.dot(twice, held_ref[s], preferred_element_type=F32)
        for cols in CHUNKS:
            gated = part_ref[half * 4 + s, here, cols] + gate_ref[half * 4 + s, here, cols] * carried[:, cols]
            put(s, cols, gated)
            squares = squares + gated * gated
    return squares


def own_half_kernel(where_ref, part_ref, gate_ref, kq_ref, held_ref, gated_ref, squares_ref):
    def body(at, carry):
        here = pl.ds(pl.multiple_of(at * TILE, TILE), TILE)

        def put(s, cols, gated):
            gated_ref[s, here, cols] = gated

        query = kq_ref[here, STATE:]
        squares_ref[here, :] = half_gated(query, held_ref, where_ref[2], here, part_ref, gate_ref, put)
        return carry

    lax.fori_loop(0, part_ref.shape[1] // TILE, body, 0)


def own_half(where, part, gate, kq, held, name, after=()):
    rows = part.shape[1]
    shapes = [((4, rows, SLAB), F32), ((rows, 128), F32)]
    return whole(own_half_kernel, where, (part, gate, kq, held), shapes, name, after)


def finish_kernel(
    length_at, where_ref, part_ref, gate_ref, kq_ref, held_ref, own_ref, squares_ref, gain_ref,
    out_ref, token_ref, gated_ref, rows_ref, sems,
):
    core = where_ref[2]

    def copy_out(at):
        here = pl.ds(pl.multiple_of(at * PART, PART), PART)
        return pltpu.make_async_copy(rows_ref.at[here], out_ref.at[here], sems.at[at])

    def body(at, carry):
        start = at * TILE
        here = pl.ds(pl.multiple_of(start, TILE), TILE)

        def put(s, cols, gated):
            gated_ref[s, :, cols] = gated

        squares = half_gated(kq_ref[here, STATE:], held_ref, 1 - core, here, part_ref, gate_ref, put)
        squares = squares + squares_ref[here, :]
        mean = jnp.sum(squares, axis=1, keepdims=True) * (1.0 / D_INNER)
        row = lax.broadcasted_iota(jnp.int32, (TILE, 1), 0) + start
        inv = jnp.where(row < where_ref[length_at], lax.rsqrt(mean + EPS), 0.0)
        for part in range(TILE // PART):
            inside = slice(part * PART, (part + 1) * PART)
            there = pl.ds(pl.multiple_of(start + part * PART, PART), PART)
            scale = jnp.broadcast_to(inv[inside], (PART, 128))
            for s in range(4):
                for cols in CHUNKS:
                    wide = pl.ds(pl.multiple_of((core * 4 + s) * SLAB + cols.start, 128), 128)
                    rows_ref[there, wide] = (own_ref[s, there, cols] * scale * gain_ref[:, wide]).astype(BF16)
                    wide = pl.ds(pl.multiple_of((4 - core * 4 + s) * SLAB + cols.start, 128), 128)
                    rows_ref[there, wide] = (gated_ref[s, inside, cols] * scale * gain_ref[:, wide]).astype(BF16)
            copy_out(at * (TILE // PART) + part).start()
        return carry

    tiles = part_ref.shape[1] // TILE
    lax.fori_loop(0, tiles, body, 0)
    token_ref[...] = jnp.zeros_like(token_ref)
    for at in range(tiles * (TILE // PART)):
        copy_out(at).wait()


def finish(where, part, gate, kq, held, own, squares, gain, length_at, name, after):
    rows = part.shape[1]
    return pl.pallas_call(
        ordered(functools.partial(finish_kernel, length_at), 8, len(after)),
        in_specs=[SMEM] + [VMEM] * (7 + len(after)),
        out_specs=[HBM, VMEM],
        scratch_shapes=[
            pltpu.VMEM((4, TILE, SLAB), F32),
            pltpu.VMEM((rows, D_INNER), BF16),
            pltpu.SemaphoreType.DMA((rows // PART,)),
        ],
        out_shape=[jax.ShapeDtypeStruct((rows, D_INNER), BF16), jax.ShapeDtypeStruct((8, 128), F32)],
        compiler_params=params(),
        cost_estimate=pl.CostEstimate(flops=1, bytes_accessed=1, transcendentals=0),
        name=name,
    )(where, part, gate, kq, held, own, squares, gain, *after)


def number(y, x, core):
    return (y % SIDE) * 2 * SIDE + (x % SIDE) * 2 + core


def moved(value, move):
    pairs = [
        (number(y, x, core), number(*move(y, x, core)))
        for y in range(SIDE)
        for x in range(SIDE)
        for core in range(2)
    ]
    return lax.ppermute(value, GROUP, pairs)


def swap_cores(value):
    return moved(value, lambda y, x, core: (y, x, 1 - core))


def along_x(value, by):
    return moved(value, lambda y, x, core: (y, x + by, core))


def round_x(here, to_next, to_opposite, to_last):
    opposite = along_x(to_opposite, 2)
    return here, along_x(to_next, 1), along_x(to_last, 3), opposite


def along_y(value, by):
    return moved(value, lambda y, x, core: (y + by, x, core))


def make_tables(where, keep, step, xbc, weight):
    shapes = [((2, HEADS, BLOCK), F32), ((2, BLOCK, 128), F32), ((2, BLOCK, 128), F32), ((SLABS, 8, SLAB), F32)]
    shapes += [(xbc.shape, BF16), (weight.shape, F32)]
    scratch = [pltpu.VMEM(keep.shape, F32), pltpu.VMEM(step.shape, F32), pltpu.SemaphoreType.DMA((7,))]
    arrays = (keep, step, xbc, weight)
    return whole(tables_kernel, where, arrays, shapes, "tables", scratch=scratch, outside=4)


def sent_states(where, xbc, weight, hist, bias, own_rows, colt, hcol):
    rows = xbc.shape[0]
    shapes = [
        ((4, rows, SLAB), BF16),
        ((rows, 2 * STATE), BF16),
        ((STATE, rows), BF16),
        ((4, STATE, SLAB), BF16),
        ((4, STATE + EXTRA, SLAB), BF16),
    ]
    scratch = [pltpu.VMEM((rows, SLAB), BF16)]
    arrays = (xbc, weight, hist, bias, own_rows, colt, hcol)
    return whole(sent_states_kernel, where, arrays, shapes, "sent_states", scratch=scratch)


def kept_states(where, xbc, weight, hist, bias, keyt, colt, hcol, after):
    rows = xbc.shape[0]
    shapes = [((4, rows, SLAB), BF16), ((4, STATE, SLAB), BF16), ((4, STATE, SLAB), F32)]
    arrays = (xbc, weight, hist, bias, keyt, colt, hcol)
    return whole(kept_states_kernel, where, arrays, shapes, "kept_states", after, [pltpu.VMEM((rows, SLAB), BF16)])


def prompt_within(where, acts, z, kq, high, col, rowt, hcol, skip, after):
    shapes = [((SLABS, z.shape[0], SLAB), F32)] * 2
    scratch = [pltpu.VMEM((2, BLOCK, BLOCK), F32)]
    arrays = (*acts, z, kq, *high, col, rowt, hcol, skip)
    return whole(prompt_within_kernel, where, arrays, shapes, "prompt_within", after, scratch)


def resp_within(where, xbc, mine, other, weight, bias, z, keep, step, skip, after):
    rows = z.shape[0]
    shapes = [((SLABS, rows, SLAB), F32)] * 2 + [((rows, 2 * STATE), BF16)]
    scratch = [
        pltpu.VMEM((HIST, D_INNER + 2 * STATE), F32),
        pltpu.VMEM((BLOCK, BLOCK), F32),
        pltpu.VMEM((HEADS, BLOCK), F32),
        pltpu.VMEM((BLOCK, 128), F32),
    ]
    arrays = (xbc, mine, other, weight, bias, z, keep, step, skip)
    return whole(resp_within_kernel, where, arrays, shapes, "resp_within", after, scratch)


def shards(
    prompt_xbc,
    prompt_z,
    prompt_step,
    prompt_keep,
    resp_xbc,
    resp_z,
    resp_step,
    resp_keep,
    resp_len,
    conv_weight,
    conv_bias,
    skip,
    gain,
):
    rows = prompt_xbc.shape[0]
    seq, core = lax.axis_index("seq"), lax.axis_index("resp")
    fixed = [seq % SIDE, seq // SIDE, core, jnp.where(lax.axis_index(GROUP) == 0, 0, 1)]
    where = jnp.stack([jnp.asarray(v, jnp.int32) for v in fixed + [rows, resp_len[0]]])
    bias_row, gain_row, skip_row = conv_bias[None, :], gain[None, :], skip[None, :]

    own_rows = prompt_xbc[rows - HIST :]
    count = 2 * SIDE * SIDE
    hist = lax.ppermute(own_rows, GROUP, [(i, i + 1) for i in range(count - 1)])
    col, rowt, colt, hcol, xbc, taps = make_tables(where, prompt_keep, prompt_step, prompt_xbc, conv_weight)
    sent_acts, kq, keyt, sent_high, msg = sent_states(
        where, xbc, taps, hist, bias_row, own_rows, colt, hcol
    )
    recv = swap_cores(msg)
    kept_acts, kept_high, own = kept_states(
        where, xbc, taps, hist, bias_row, keyt, colt, hcol, after=(msg,)
    )
    with_extra = ((STATE + EXTRA, SLAB), BF16)
    c0, c1, c2, c3 = whole(chip_kernel, where, (own, recv, hcol, own_rows), [with_extra] * 4, "chip")
    pieces = round_x(c0, c1, c2, c3)
    part, gate = prompt_within(
        where, (sent_acts, kept_acts), prompt_z, kq, (sent_high, kept_high), col, rowt, hcol, skip_row,
        after=(c1, c2, c3),
    )
    (total,) = whole(row_kernel, where, pieces, [with_extra], "row", after=(part, gate), scratch=[pltpu.VMEM((STATE, SLAB), F32)])
    opposite = along_y(total, 2)
    totals = (total, along_y(total, 1), along_y(total, 3), opposite)
    e0, e1, e2, e3, final, tail = whole(
        entering_kernel, where, totals + pieces, [with_extra] * 5 + [((EXTRA, SLAB), BF16)], "entering", after=(part, gate),
        scratch=[pltpu.VMEM((SIDE + 1, STATE, SLAB), F32)],
    )
    tail_other = swap_cores(tail)
    back = round_x(e0, e1, e2, e3)
    finals = round_x(final, final, final, final)
    resp_part, resp_gate, resp_kq = resp_within(
        where, resp_xbc[0], tail, tail_other, conv_weight, bias_row, resp_z[0],
        resp_keep.reshape(HEADS, BLOCK), resp_step.reshape(HEADS, BLOCK), skip_row, after=(e1, e2, e3),
    )
    four = ((4, 2 * STATE, SLAB), BF16)
    mine, send, final_mine = whole(
        cores_kernel,
        where,
        back + finals + (own, recv, hcol),
        [four] * 3,
        "cores",
        after=(resp_part, resp_gate, part, gate),
    )
    other, final_other = swap_cores(send), swap_cores(final_mine)
    gated, squares = own_half(where, part, gate, kq, mine, "prompt_own_half", after=(send,))
    resp_gated, resp_squares = own_half(
        where, resp_part, resp_gate, resp_kq, final_mine, "resp_own_half", after=(squares,)
    )
    prompt_out, token = finish(
        where, part, gate, kq, other, gated, squares, gain_row, 4, "prompt_finish", after=(resp_squares,)
    )
    resp_out, _ = finish(
        where, resp_part, resp_gate, resp_kq, final_other, resp_gated, resp_squares, gain_row, 5, "resp_finish",
        after=(token,),
    )
    return (prompt_out, resp_out[None])


def solution(mesh):
    return jax.shard_map(
        shards,
        mesh=mesh,
        in_specs=(
            P(("grp", "seq", "resp"), None),
            P(("grp", "seq", "resp"), None),
            P(None, ("grp", "seq", "resp")),
            P(None, ("grp", "seq", "resp")),
            P(("grp", "seq", "resp"), None, None),
            P(("grp", "seq", "resp"), None, None),
            P(None, ("grp", "seq", "resp"), None),
            P(None, ("grp", "seq", "resp"), None),
            P(("grp", "seq", "resp")),
            P(),
            P(),
            P(),
            P(),
        ),
        out_specs=(P(("grp", "seq", "resp"), None), P(("grp", "seq", "resp"), None, None)),
        check_vma=False,
    )
```

```python
import functools

import jax
import jax.numpy as jnp
from jax import lax
from jax.experimental import pallas as pl
from jax.experimental.pallas import tpu as pltpu
from jax.sharding import PartitionSpec as P

HEADS = 80
HEAD_DIM = 64
STATE = 128
KERNEL = 4
BLOCK = 128
D_INNER = 5120
SLABS = 8
SLAB = D_INNER // SLABS
SLAB_HEADS = HEADS // SLABS
PAIRS = SLAB // 128
EXTRA = 16
HIST = 8
HALF_TAIL = (D_INNER + 2 * STATE) // 2
PIECES = -(-HALF_TAIL // SLAB)
EPS = 1e-05
GROUP = ("seq", "resp")
SIDE = 4

F32 = jnp.float32
BF16 = jnp.bfloat16


SMEM = pl.BlockSpec(memory_space=pltpu.SMEM)
VMEM = pl.BlockSpec(memory_space=pltpu.VMEM)
HBM = pl.BlockSpec(memory_space=pltpu.HBM)


def ordered(kernel, inputs, extra):
    def body(*refs):
        kernel(*refs[:inputs], *refs[inputs + extra :])

    return body


def params(mib=12):
    return pltpu.CompilerParams(vmem_limit_bytes=mib * 2**20)


def whole(kernel, where, arrays, shapes, name, after=(), scratch=(), outside=0):
    return pl.pallas_call(
        ordered(kernel, 1 + len(arrays), len(after)),
        in_specs=[SMEM] + [HBM] * outside + [VMEM] * (len(arrays) - outside + len(after)),
        out_specs=[VMEM] * len(shapes),
        out_shape=[jax.ShapeDtypeStruct(shape, dtype) for shape, dtype in shapes],
        scratch_shapes=list(scratch),
        compiler_params=params(),
        cost_estimate=pl.CostEstimate(flops=1, bytes_accessed=1, transcendentals=0),
        name=name,
    )(where, *(pltpu.with_memory_space_constraint(a, pltpu.HBM) for a in arrays[:outside]), *arrays[outside:], *after)


def silu(value):
    return 0.5 * value * (1.0 + jnp.tanh(0.5 * value))


def spread(table, pair):
    lane = lax.broadcasted_iota(jnp.int32, table.shape, 1)
    return jnp.take_along_axis(table, 2 * pair + lane // HEAD_DIM, axis=1, mode="promise_in_bounds")


def row_of_heads(ref, shift):
    row = jnp.concatenate([ref[...], jnp.zeros((1, 128 - HEADS), F32)], axis=1)
    return pltpu.roll(jnp.broadcast_to(row, (8, 128)), shift, 1)


def first_part(shape):
    return lax.broadcasted_iota(jnp.int32, shape, 1) % HEAD_DIM < HEAD_DIM // 2


def extra_rows(decay, tail):
    wide = jnp.broadcast_to(decay, tail.shape)
    high = wide.astype(BF16).astype(F32)
    coded = jnp.where(first_part(tail.shape), high, wide - high)
    return jnp.where(lax.broadcasted_iota(jnp.int32, tail.shape, 0) == 0, coded, tail).astype(BF16)


def decay_of(rows):
    wide = rows.astype(F32)
    half = HEAD_DIM // 2
    other = jnp.where(first_part(wide.shape), pltpu.roll(wide, SLAB - half, 1), pltpu.roll(wide, half, 1))
    return (wide + other)[0:1]


def tail_rows(rows_ref, half):
    block = jnp.zeros((EXTRA, SLAB), F32)
    place = lax.broadcasted_iota(jnp.int32, block.shape, 0)
    for piece in range(PIECES):
        width = min(SLAB, HALF_TAIL - piece * SLAB)
        start = pl.multiple_of(half * HALF_TAIL + piece * SLAB, 128)
        wide = rows_ref[:, pl.ds(start, width)].astype(F32)
        if width < SLAB:
            wide = jnp.concatenate([wide, jnp.zeros((HIST, SLAB - width), F32)], axis=1)
        for row in range(KERNEL - 1):
            line = wide[HIST - (KERNEL - 1) + row : HIST - (KERNEL - 1) + row + 1]
            block = jnp.where(place == 1 + PIECES * row + piece, line, block)
    return block


def block_table(keep, step):
    lane = lax.broadcasted_iota(jnp.int32, (HEADS, BLOCK), 1)
    cum = keep
    for by in (1, 2, 4, 8, 16, 32, 64):
        cum = cum + jnp.where(lane >= by, pltpu.roll(cum, by, 1), 0.0)
    gap = cum - 0.5 * cum[:, BLOCK - 1 : BLOCK]
    col = jnp.exp(-gap) * step
    blank = jnp.zeros((128 - HEADS, BLOCK), F32)
    return col, jnp.concatenate([jnp.exp(gap), blank], axis=0).T, jnp.concatenate([col, blank], axis=0).T


def tables_kernel(
    where_ref, keep_from, step_from, x_from, w_from, col_ref, rowt_ref, colt_ref, hcol_ref, x_ref, w_ref,
    keep_ref, step_ref, sems,
):
    copies = [
        pltpu.make_async_copy(keep_from, keep_ref, sems.at[0]),
        pltpu.make_async_copy(step_from, step_ref, sems.at[1]),
        pltpu.make_async_copy(w_from, w_ref, sems.at[2]),
    ]
    share = x_ref.shape[0] // 4
    for at in range(4):
        rows = pl.ds(at * share, share)
        copies.append(pltpu.make_async_copy(x_from.at[rows], x_ref.at[rows], sems.at[3 + at]))
    for copy in copies:
        copy.start()
    for copy in copies[:2]:
        copy.wait()
    place = lax.broadcasted_iota(jnp.int32, (8, 128), 0)
    stack = jnp.zeros((8, 128), F32)
    for block in range(2):
        here = slice(block * BLOCK, (block + 1) * BLOCK)
        col_ref[block], rowt, colt_ref[block] = block_table(keep_ref[:, here], step_ref[:, here])
        rowt_ref[block] = rowt
        stack = jnp.where(place == block, rowt[BLOCK - 1 : BLOCK], stack)
    for pair in range(HEADS // 2):
        at = (pair % PAIRS) * 128
        hcol_ref[pair // PAIRS, :, at : at + 128] = spread(stack, pair)
    for copy in copies[2:]:
        copy.wait()


def conv_columns(rows, hist, weight, bias):
    wide = jnp.concatenate([hist, rows.astype(F32)], axis=0)
    total = bias + weight[KERNEL - 1 : KERNEL] * wide
    for back in range(1, KERNEL):
        total = total + weight[KERNEL - 1 - back : KERNEL - back] * pltpu.roll(wide, back, 0)
    return silu(total[HIST:]).astype(BF16)


def add_states(slab, at, conv, colt_ref, hcol_ref, keyt_ref, acts_ref, high_ref, weighted_ref, put):
    shift = lax.rem(128 - SLAB_HEADS * slab, 128)
    colts = [pltpu.roll(colt_ref[block], shift, 1) for block in range(2)]
    for pair in range(PAIRS):
        cols = slice(pair * 128, pair * 128 + 128)
        acts = conv(pl.ds(pl.multiple_of(slab * SLAB + pair * 128, 128), 128))
        acts_ref[at, :, cols] = acts
        for block in range(2):
            here = slice(block * BLOCK, (block + 1) * BLOCK)
            weight = spread(colts[block], pair) * hcol_ref[slab, block : block + 1, cols]
            weighted_ref[here, cols] = (acts[here].astype(F32) * weight).astype(BF16)
    first = jnp.dot(keyt_ref[:, 0:BLOCK], weighted_ref[0:BLOCK], preferred_element_type=F32)
    second = jnp.dot(keyt_ref[:, BLOCK:], weighted_ref[BLOCK:], preferred_element_type=F32)
    high_ref[at] = first.astype(BF16)
    put(hcol_ref[slab, 1:2] ** 2 * first + second)


def convolver(where_ref, x_ref, hist_ref, w_ref, b_ref):
    keep_history = where_ref[3].astype(F32)

    def conv(cols):
        hist = hist_ref[:, cols].astype(F32) * keep_history
        return conv_columns(x_ref[:, cols], hist, w_ref[:, cols], b_ref[:, cols])

    return conv


def sent_states_kernel(
    where_ref, x_ref, w_ref, hist_ref, b_ref, rows_ref, colt_ref, hcol_ref,
    acts_ref, kq_ref, keyt_ref, high_ref, msg_ref, weighted_ref,
):
    half = 1 - where_ref[2]
    conv = convolver(where_ref, x_ref, hist_ref, w_ref, b_ref)
    key = conv(slice(D_INNER, D_INNER + STATE))
    kq_ref[:, 0:STATE] = key
    kq_ref[:, STATE : 2 * STATE] = conv(slice(D_INNER + STATE, D_INNER + 2 * STATE))
    keyt_ref[...] = key.astype(F32).T.astype(BF16)

    def body(at, carry):
        slab = half * 4 + at

        def put(state):
            msg_ref[at, 0:STATE] = state.astype(BF16)

        add_states(slab, at, conv, colt_ref, hcol_ref, keyt_ref, acts_ref, high_ref, weighted_ref, put)
        decay = (hcol_ref[slab, 0:1] * hcol_ref[slab, 1:2]) ** 2
        msg_ref[at, STATE:] = extra_rows(decay, jnp.zeros((EXTRA, SLAB), F32))
        return carry

    lax.fori_loop(0, 4, body, 0)
    slab = half * 4
    decay = (hcol_ref[slab, 0:1] * hcol_ref[slab, 1:2]) ** 2
    msg_ref[0, STATE:] = extra_rows(decay, tail_rows(rows_ref, half))


def kept_states_kernel(
    where_ref, x_ref, w_ref, hist_ref, b_ref, keyt_ref, colt_ref, hcol_ref, acts_ref, high_ref, own_ref, weighted_ref
):
    half = where_ref[2]
    conv = convolver(where_ref, x_ref, hist_ref, w_ref, b_ref)

    def body(at, carry):
        def put(state):
            own_ref[at] = state

        add_states(half * 4 + at, at, conv, colt_ref, hcol_ref, keyt_ref, acts_ref, high_ref, weighted_ref, put)
        return carry

    lax.fori_loop(0, 4, body, 0)


def masked_scores(key_query):
    scores = lax.dot_general(
        key_query[:, STATE:], key_query[:, :STATE], (((1,), (1,)), ((), ())), preferred_element_type=F32
    )
    row = lax.broadcasted_iota(jnp.int32, (BLOCK, BLOCK), 0)
    col = lax.broadcasted_iota(jnp.int32, (BLOCK, BLOCK), 1)
    return jnp.where(row >= col, scores, 0.0)


def within_pair(scores, col_rows, values):
    mixes = [(scores * row).astype(BF16) for row in col_rows]
    first = lax.broadcasted_iota(jnp.int32, (BLOCK, 128), 1) < HEAD_DIM
    wide = values.astype(F32)
    stacked = jnp.concatenate(
        [jnp.where(first, wide, 0.0).astype(BF16), jnp.where(first, 0.0, wide).astype(BF16)], axis=0
    )
    return jnp.dot(jnp.concatenate(mixes, axis=1), stacked, preferred_element_type=F32)


def prompt_within_kernel(
    where_ref, sent_acts, kept_acts, z_ref, kq_ref, sent_high, kept_high, col_ref, rowt_ref, hcol_ref, skip_ref,
    part_ref, gate_ref, scores_ref,
):
    for block in range(2):
        scores_ref[block] = masked_scores(kq_ref[block * BLOCK : (block + 1) * BLOCK, :])

    def step(half, acts_ref, high_ref, at, carry):
        slab = half * 4 + at
        shift = lax.rem(128 - SLAB_HEADS * slab, 128)
        rowts = [pltpu.roll(rowt_ref[block], shift, 1) for block in range(2)]
        skips = row_of_heads(skip_ref, shift)
        earlier = jnp.dot(kq_ref[BLOCK : 2 * BLOCK, STATE:], high_ref[at], preferred_element_type=F32)
        for pair in range(PAIRS):
            cols = slice(pair * 128, pair * 128 + 128)
            gate_cols = pl.ds(pl.multiple_of(slab * SLAB + pair * 128, 128), 128)
            first_half = hcol_ref[slab, 0:1, cols]
            second_half = hcol_ref[slab, 1:2, cols]
            skip = spread(skips, pair)[0:1]
            head = slab * SLAB_HEADS + 2 * pair
            for block in range(2):
                here = slice(block * BLOCK, (block + 1) * BLOCK)
                values = acts_ref[at, here, cols]
                col_rows = [col_ref[block, pl.ds(head + which, 1), :] for which in range(2)]
                mixed = within_pair(scores_ref[block], col_rows, values)
                scale = first_half
                if block == 1:
                    mixed += second_half * earlier[:, cols]
                    scale = second_half * first_half * first_half
                gate = silu(z_ref[here, gate_cols].astype(F32))
                row = spread(rowts[block], pair)
                part_ref[slab, here, cols] = (row * mixed + skip * values.astype(F32)) * gate
                gate_ref[slab, here, cols] = row * scale * gate
        return carry

    core = where_ref[2]
    lax.fori_loop(0, 4, functools.partial(step, 1 - core, sent_acts, sent_high), 0)
    lax.fori_loop(0, 4, functools.partial(step, core, kept_acts, kept_high), 0)


def resp_within_kernel(
    where_ref, x_ref, mine_ref, other_ref, w_ref, b_ref, z_ref, keep_ref, step_ref, skip_ref,
    part_ref, gate_ref, kq_ref, hist_ref, scores_ref, col_ref, rowt_ref,
):
    core = where_ref[2]
    for half in range(2):
        flag = (core == half).astype(F32)
        tail = mine_ref[...].astype(F32) * flag + other_ref[...].astype(F32) * (1.0 - flag)
        for piece in range(PIECES):
            width = min(SLAB, HALF_TAIL - piece * SLAB)
            start = half * HALF_TAIL + piece * SLAB
            block = jnp.zeros((HIST, SLAB), F32)
            place = lax.broadcasted_iota(jnp.int32, block.shape, 0)
            for row in range(KERNEL - 1):
                at = 1 + PIECES * row + piece
                block = jnp.where(place == HIST - (KERNEL - 1) + row, tail[at : at + 1], block)
            hist_ref[:, start : start + width] = block[:, 0:width]
    col_ref[...], rowt_ref[...], _ = block_table(keep_ref[...], step_ref[...])

    def conv(cols):
        return conv_columns(x_ref[:, cols], hist_ref[:, cols], w_ref[:, cols], b_ref[:, cols])

    for at in (0, STATE):
        kq_ref[:, at : at + STATE] = conv(slice(D_INNER + at, D_INNER + at + STATE))
    scores_ref[...] = masked_scores(kq_ref[...])

    def step(slab, carry):
        shift = lax.rem(128 - SLAB_HEADS * slab, 128)
        rowt = pltpu.roll(rowt_ref[...], shift, 1)
        skips = row_of_heads(skip_ref, shift)
        for pair in range(PAIRS):
            cols = slice(pair * 128, pair * 128 + 128)
            wide_cols = pl.ds(pl.multiple_of(slab * SLAB + pair * 128, 128), 128)
            values = conv(wide_cols)
            head = slab * SLAB_HEADS + 2 * pair
            col_rows = [col_ref[pl.ds(head + which, 1), :] for which in range(2)]
            mixed = within_pair(scores_ref[...], col_rows, values)
            gate = silu(z_ref[:, wide_cols].astype(F32))
            row = spread(rowt, pair)
            half = row[BLOCK - 1 : BLOCK]
            part_ref[slab, :, cols] = (row * mixed + spread(skips, pair)[0:1] * values.astype(F32)) * gate
            gate_ref[slab, :, cols] = row * half * gate
        return carry

    lax.fori_loop(0, SLABS, step, 0)


def at_shift(place, by):
    return lax.rem(place + by + SIDE, SIDE)


def pick(condition, value):
    flag = condition.astype(F32)
    return value * flag + (1.0 - flag)


CHUNKS = [slice(at, at + 128) for at in range(0, SLAB, 128)]


def chip_kernel(where_ref, own_ref, recv_ref, hcol_ref, rows_ref, *out_refs):
    x, core = where_ref[0], where_ref[2]
    first = (core == 0).astype(F32)
    tail = tail_rows(rows_ref, core) * (1.0 - first) + recv_ref[0, STATE:, :].astype(F32) * first
    for shift in range(SIDE):
        slab = at_shift(x, shift)
        half = hcol_ref[core * 4 + slab]
        mine = (half[0:1] * half[1:2]) ** 2
        theirs = decay_of(recv_ref[slab, STATE:, :])
        own_scale = theirs * first + (1.0 - first)
        recv_scale = mine * (1.0 - first) + first
        for cols in CHUNKS:
            received = recv_ref[slab, 0:STATE, cols].astype(F32)
            state = own_scale[:, cols] * own_ref[slab, :, cols] + recv_scale[:, cols] * received
            out_refs[shift][0:STATE, cols] = state.astype(BF16)
        out_refs[shift][STATE:] = extra_rows(mine * theirs, tail)


def weights_to(places, decays, target):
    ones = jnp.ones((1, SLAB), F32)
    weights = []
    for i in range(SIDE):
        scale = (places[i] < target).astype(F32) * ones
        for k in range(SIDE):
            if k != i:
                between = jnp.logical_and(places[k] > places[i], places[k] < target)
                scale = scale * pick(between, decays[k])
        weights.append(scale)
    through = ones
    for k in range(SIDE):
        through = through * pick(places[k] < target, decays[k])
    return weights, through


def weighted_sum(weights, refs, cols):
    return sum(w[:, cols] * ref[0:STATE, cols].astype(F32) for w, ref in zip(weights, refs))


def last_tail(places, refs):
    return sum(ref[STATE:].astype(F32) * (place == SIDE - 1).astype(F32) for place, ref in zip(places, refs))


def direction(state_ref):
    total = jnp.zeros((STATE, 128), F32)
    for cols in CHUNKS:
        state = state_ref[:, cols]
        total = total + state * jnp.sum(state, axis=0, keepdims=True)
    along = jnp.sum(total, axis=1, keepdims=True)
    along = along * (1.0 / (jnp.max(jnp.abs(along)) + 1e-30))
    along = jnp.broadcast_to(along.astype(BF16).astype(F32), (STATE, 128))
    return along, jnp.sum(along * along, axis=0, keepdims=True) + 1e-30


def split_off(state_ref, along, square, out_ref):
    highs, lows = [], []
    for cols in CHUNKS:
        state = state_ref[:, cols]
        factor = jnp.sum(state * along, axis=0, keepdims=True) / square
        high = factor.astype(BF16).astype(F32)
        low = (factor - high).astype(BF16).astype(F32)
        out_ref[0:STATE, cols] = (state - along * (high + low)).astype(BF16)
        highs.append(high)
        lows.append(low)
    return highs, lows


def as_columns(row):
    return jnp.broadcast_to(row, (STATE, 128)).T


def joined(ref, along, factor, cols):
    return ref[0:STATE, cols].astype(F32) + along * factor[:, cols]


def row_kernel(where_ref, r0, r1, r3, r2, out_ref, state_ref):
    refs = (r0, r1, r2, r3)
    places = [at_shift(where_ref[0], -i) for i in range(SIDE)]
    weights, through = weights_to(places, [decay_of(ref[STATE:]) for ref in refs], SIDE)
    for cols in CHUNKS:
        state_ref[:, cols] = weighted_sum(weights, refs, cols)
    along, square = direction(state_ref)
    highs, lows = split_off(state_ref, along, square, out_ref)
    tail = last_tail(places, refs)
    blank = jnp.zeros((1, 128), F32)
    lines = [
        jnp.concatenate([blank] + highs[:4], axis=1),
        jnp.concatenate([blank] + lows[:4], axis=1),
        jnp.concatenate([blank, highs[4], lows[4], along.T[0:1], blank], axis=1),
    ]
    place = lax.broadcasted_iota(jnp.int32, tail.shape, 0)
    for row, line in enumerate(lines):
        tail = tail + jnp.where(place == PIECES * (row + 1), line, 0.0)
    out_ref[STATE:] = extra_rows(through, tail)


def entering_kernel(where_ref, t0, t1, t3, t2, r0, r1, r3, r2, e0, e1, e2, e3, final_ref, tail_ref, state_ref):
    x, y = where_ref[0], where_ref[1]
    refs, totals, outs = (r0, r1, r2, r3), (t0, t1, t2, t3), (e0, e1, e2, e3)
    rows = [at_shift(y, -i) for i in range(SIDE)]
    row_decays = [decay_of(ref[STATE:]) for ref in totals]
    to_end, _ = weights_to(rows, row_decays, SIDE)
    to_row, _ = weights_to(rows, row_decays, y)
    places = [at_shift(x, -i) for i in range(SIDE)]
    decays = [decay_of(ref[STATE:]) for ref in refs]
    to_chips = [weights_to(places, decays, at_shift(x, shift)) for shift in range(SIDE)]
    coded = []
    for ref in totals:
        wide = ref[STATE:].astype(F32)
        high = jnp.concatenate([wide[PIECES : PIECES + 1, 128:], wide[3 * PIECES : 3 * PIECES + 1, 128:256]], axis=1)
        low = jnp.concatenate(
            [wide[2 * PIECES : 2 * PIECES + 1, 128:], wide[3 * PIECES : 3 * PIECES + 1, 256:384]], axis=1
        )
        coded.append((as_columns(wide[3 * PIECES : 3 * PIECES + 1, 384:512]), high + low))
    for cols in CHUNKS:
        states = [joined(ref, along, factor, cols) for ref, (along, factor) in zip(totals, coded)]
        state_ref[SIDE, :, cols] = sum(w[:, cols] * state for w, state in zip(to_end, states))
        row_in = sum(w[:, cols] * state for w, state in zip(to_row, states))
        for shift, (weights, through) in enumerate(to_chips):
            state_ref[shift, :, cols] = through[:, cols] * row_in + weighted_sum(weights, refs, cols)
    along, square = direction(state_ref.at[SIDE])
    line = jnp.concatenate([along.T[0:1], jnp.zeros((1, SLAB - 128), F32)], axis=1)
    place = lax.broadcasted_iota(jnp.int32, (EXTRA, SLAB), 0)
    for at, out in enumerate(outs + (final_ref,)):
        highs, lows = split_off(state_ref.at[at], along, square, out)
        block = jnp.where(place == 0, jnp.concatenate(highs, axis=1), jnp.where(place == 1, jnp.concatenate(lows, axis=1), 0.0))
        out[STATE:] = jnp.where(place == 2, line, block).astype(BF16)
    tail_ref[...] = last_tail(rows, totals).astype(BF16)


def put_pair(ref, slab, cols, state):
    high = state.astype(BF16)
    ref[slab, 0:STATE, cols] = high
    ref[slab, STATE:, cols] = (state - high.astype(F32)).astype(BF16)


def uncoded(ref):
    wide = ref[STATE:].astype(F32)
    return as_columns(wide[2:3, 0:128]), wide[0:1] + wide[1:2]


def cores_kernel(
    where_ref, g0, g1, g3, g2, own_ref, recv_ref, hcol_ref, mine_ref, send_ref
):
    x, core = where_ref[0], where_ref[2]
    first = (core == 0).astype(F32)
    last = 1.0 - first
    for i, ref in enumerate((g0, g1, g2, g3)):
        slab = at_shift(x, -i)
        half = hcol_ref[core * 4 + slab]
        mine = (half[0:1] * half[1:2]) ** 2
        decay = mine * first + decay_of(recv_ref[slab, STATE:, :]) * last
        along, factor = uncoded(ref)
        for cols in CHUNKS:
            earlier = own_ref[slab, :, cols] * first + recv_ref[slab, 0:STATE, cols].astype(F32) * last
            start = joined(ref, along, factor, cols)
            later = decay[:, cols] * start + earlier
            put_pair(mine_ref, slab, cols, start * first + later * last)
            put_pair(send_ref, slab, cols, later * first + start * last)


def final_kernel(where_ref, f0, f1, f3, f2, final_ref):
    for i, ref in enumerate((f0, f1, f2, f3)):
        slab = at_shift(where_ref[0], -i)
        along, factor = uncoded(ref)
        for cols in CHUNKS:
            put_pair(final_ref, slab, cols, joined(ref, along, factor, cols))


TILE = 128
PART = 32


def half_gated(query, held_ref, half, here, part_ref, gate_ref, put):
    squares = jnp.zeros((TILE, 128), F32)
    twice = jnp.concatenate([query, query], axis=1)
    for s in range(4):
        carried = jnp.dot(twice, held_ref[s], preferred_element_type=F32)
        for cols in CHUNKS:
            gated = part_ref[half * 4 + s, here, cols] + gate_ref[half * 4 + s, here, cols] * carried[:, cols]
            put(s, cols, gated)
            squares = squares + gated * gated
    return squares


def own_half_kernel(where_ref, part_ref, gate_ref, kq_ref, held_ref, gated_ref, squares_ref):
    def body(at, carry):
        here = pl.ds(pl.multiple_of(at * TILE, TILE), TILE)

        def put(s, cols, gated):
            gated_ref[s, here, cols] = gated

        query = kq_ref[here, STATE:]
        squares_ref[here, :] = half_gated(query, held_ref, where_ref[2], here, part_ref, gate_ref, put)
        return carry

    lax.fori_loop(0, part_ref.shape[1] // TILE, body, 0)


def own_half(where, part, gate, kq, held, name, after=()):
    rows = part.shape[1]
    shapes = [((4, rows, SLAB), F32), ((rows, 128), F32)]
    return whole(own_half_kernel, where, (part, gate, kq, held), shapes, name, after)


def finish_kernel(
    length_at, where_ref, part_ref, gate_ref, kq_ref, held_ref, own_ref, squares_ref, gain_ref,
    out_ref, token_ref, gated_ref, rows_ref, sems,
):
    core = where_ref[2]

    def copy_out(at):
        here = pl.ds(pl.multiple_of(at * PART, PART), PART)
        return pltpu.make_async_copy(rows_ref.at[here], out_ref.at[here], sems.at[at])

    def body(at, carry):
        start = at * TILE
        here = pl.ds(pl.multiple_of(start, TILE), TILE)

        def put(s, cols, gated):
            gated_ref[s, :, cols] = gated

        squares = half_gated(kq_ref[here, STATE:], held_ref, 1 - core, here, part_ref, gate_ref, put)
        squares = squares + squares_ref[here, :]
        mean = jnp.sum(squares, axis=1, keepdims=True) * (1.0 / D_INNER)
        row = lax.broadcasted_iota(jnp.int32, (TILE, 1), 0) + start
        inv = jnp.where(row < where_ref[length_at], lax.rsqrt(mean + EPS), 0.0)
        for part in range(TILE // PART):
            inside = slice(part * PART, (part + 1) * PART)
            there = pl.ds(pl.multiple_of(start + part * PART, PART), PART)
            scale = jnp.broadcast_to(inv[inside], (PART, 128))
            for s in range(4):
                for cols in CHUNKS:
                    wide = pl.ds(pl.multiple_of((core * 4 + s) * SLAB + cols.start, 128), 128)
                    rows_ref[there, wide] = (own_ref[s, there, cols] * scale * gain_ref[:, wide]).astype(BF16)
                    wide = pl.ds(pl.multiple_of((4 - core * 4 + s) * SLAB + cols.start, 128), 128)
                    rows_ref[there, wide] = (gated_ref[s, inside, cols] * scale * gain_ref[:, wide]).astype(BF16)
            copy_out(at * (TILE // PART) + part).start()
        return carry

    tiles = part_ref.shape[1] // TILE
    lax.fori_loop(0, tiles, body, 0)
    token_ref[...] = jnp.zeros_like(token_ref)
    for at in range(tiles * (TILE // PART)):
        copy_out(at).wait()


def finish(where, part, gate, kq, held, own, squares, gain, length_at, name, after):
    rows = part.shape[1]
    return pl.pallas_call(
        ordered(functools.partial(finish_kernel, length_at), 8, len(after)),
        in_specs=[SMEM] + [VMEM] * (7 + len(after)),
        out_specs=[HBM, VMEM],
        scratch_shapes=[
            pltpu.VMEM((4, TILE, SLAB), F32),
            pltpu.VMEM((rows, D_INNER), BF16),
            pltpu.SemaphoreType.DMA((rows // PART,)),
        ],
        out_shape=[jax.ShapeDtypeStruct((rows, D_INNER), BF16), jax.ShapeDtypeStruct((8, 128), F32)],
        compiler_params=params(),
        cost_estimate=pl.CostEstimate(flops=1, bytes_accessed=1, transcendentals=0),
        name=name,
    )(where, part, gate, kq, held, own, squares, gain, *after)


def number(y, x, core):
    return (y % SIDE) * 2 * SIDE + (x % SIDE) * 2 + core


def moved(value, move):
    pairs = [
        (number(y, x, core), number(*move(y, x, core)))
        for y in range(SIDE)
        for x in range(SIDE)
        for core in range(2)
    ]
    return lax.ppermute(value, GROUP, pairs)


def swap_cores(value):
    return moved(value, lambda y, x, core: (y, x, 1 - core))


def along_x(value, by):
    return moved(value, lambda y, x, core: (y, x + by, core))


def round_x(here, to_next, to_opposite, to_last):
    opposite = along_x(to_opposite, 2)
    return here, along_x(to_next, 1), along_x(to_last, 3), opposite


def along_y(value, by):
    return moved(value, lambda y, x, core: (y + by, x, core))


def make_tables(where, keep, step, xbc, weight):
    shapes = [((2, HEADS, BLOCK), F32), ((2, BLOCK, 128), F32), ((2, BLOCK, 128), F32), ((SLABS, 8, SLAB), F32)]
    shapes += [(xbc.shape, BF16), (weight.shape, F32)]
    scratch = [pltpu.VMEM(keep.shape, F32), pltpu.VMEM(step.shape, F32), pltpu.SemaphoreType.DMA((7,))]
    arrays = (keep, step, xbc, weight)
    return whole(tables_kernel, where, arrays, shapes, "tables", scratch=scratch, outside=4)


def sent_states(where, xbc, weight, hist, bias, own_rows, colt, hcol):
    rows = xbc.shape[0]
    shapes = [
        ((4, rows, SLAB), BF16),
        ((rows, 2 * STATE), BF16),
        ((STATE, rows), BF16),
        ((4, STATE, SLAB), BF16),
        ((4, STATE + EXTRA, SLAB), BF16),
    ]
    scratch = [pltpu.VMEM((rows, SLAB), BF16)]
    arrays = (xbc, weight, hist, bias, own_rows, colt, hcol)
    return whole(sent_states_kernel, where, arrays, shapes, "sent_states", scratch=scratch)


def kept_states(where, xbc, weight, hist, bias, keyt, colt, hcol, after):
    rows = xbc.shape[0]
    shapes = [((4, rows, SLAB), BF16), ((4, STATE, SLAB), BF16), ((4, STATE, SLAB), F32)]
    arrays = (xbc, weight, hist, bias, keyt, colt, hcol)
    return whole(kept_states_kernel, where, arrays, shapes, "kept_states", after, [pltpu.VMEM((rows, SLAB), BF16)])


def prompt_within(where, acts, z, kq, high, col, rowt, hcol, skip, after):
    shapes = [((SLABS, z.shape[0], SLAB), F32)] * 2
    scratch = [pltpu.VMEM((2, BLOCK, BLOCK), F32)]
    arrays = (*acts, z, kq, *high, col, rowt, hcol, skip)
    return whole(prompt_within_kernel, where, arrays, shapes, "prompt_within", after, scratch)


def resp_within(where, xbc, mine, other, weight, bias, z, keep, step, skip, after):
    rows = z.shape[0]
    shapes = [((SLABS, rows, SLAB), F32)] * 2 + [((rows, 2 * STATE), BF16)]
    scratch = [
        pltpu.VMEM((HIST, D_INNER + 2 * STATE), F32),
        pltpu.VMEM((BLOCK, BLOCK), F32),
        pltpu.VMEM((HEADS, BLOCK), F32),
        pltpu.VMEM((BLOCK, 128), F32),
    ]
    arrays = (xbc, mine, other, weight, bias, z, keep, step, skip)
    return whole(resp_within_kernel, where, arrays, shapes, "resp_within", after, scratch)


def shards(
    prompt_xbc,
    prompt_z,
    prompt_step,
    prompt_keep,
    resp_xbc,
    resp_z,
    resp_step,
    resp_keep,
    resp_len,
    conv_weight,
    conv_bias,
    skip,
    gain,
):
    rows = prompt_xbc.shape[0]
    seq, core = lax.axis_index("seq"), lax.axis_index("resp")
    fixed = [seq % SIDE, seq // SIDE, core, jnp.where(lax.axis_index(GROUP) == 0, 0, 1)]
    where = jnp.stack([jnp.asarray(v, jnp.int32) for v in fixed + [rows, resp_len[0]]])
    bias_row, gain_row, skip_row = conv_bias[None, :], gain[None, :], skip[None, :]

    own_rows = prompt_xbc[rows - HIST :]
    count = 2 * SIDE * SIDE
    hist = lax.ppermute(own_rows, GROUP, [(i, i + 1) for i in range(count - 1)])
    col, rowt, colt, hcol, xbc, taps = make_tables(where, prompt_keep, prompt_step, prompt_xbc, conv_weight)
    sent_acts, kq, keyt, sent_high, msg = sent_states(
        where, xbc, taps, hist, bias_row, own_rows, colt, hcol
    )
    recv = swap_cores(msg)
    kept_acts, kept_high, own = kept_states(
        where, xbc, taps, hist, bias_row, keyt, colt, hcol, after=(msg,)
    )
    with_extra = ((STATE + EXTRA, SLAB), BF16)
    c0, c1, c2, c3 = whole(chip_kernel, where, (own, recv, hcol, own_rows), [with_extra] * 4, "chip")
    pieces = round_x(c0, c1, c2, c3)
    part, gate = prompt_within(
        where, (sent_acts, kept_acts), prompt_z, kq, (sent_high, kept_high), col, rowt, hcol, skip_row,
        after=(c1, c2, c3),
    )
    (total,) = whole(row_kernel, where, pieces, [with_extra], "row", after=(part, gate), scratch=[pltpu.VMEM((STATE, SLAB), F32)])
    opposite = along_y(total, 2)
    totals = (total, along_y(total, 1), along_y(total, 3), opposite)
    e0, e1, e2, e3, final, tail = whole(
        entering_kernel, where, totals + pieces, [with_extra] * 5 + [((EXTRA, SLAB), BF16)], "entering", after=(part, gate),
        scratch=[pltpu.VMEM((SIDE + 1, STATE, SLAB), F32)],
    )
    tail_other = swap_cores(tail)
    back = round_x(e0, e1, e2, e3)
    finals = round_x(final, final, final, final)
    resp_part, resp_gate, resp_kq = resp_within(
        where, resp_xbc[0], tail, tail_other, conv_weight, bias_row, resp_z[0],
        resp_keep.reshape(HEADS, BLOCK), resp_step.reshape(HEADS, BLOCK), skip_row, after=(e1, e2, e3),
    )
    four = ((4, 2 * STATE, SLAB), BF16)
    mine, send = whole(
        cores_kernel, where, back + (own, recv, hcol), [four] * 2, "cores", after=(resp_part, resp_gate, part, gate)
    )
    other = swap_cores(send)
    gated, squares = own_half(where, part, gate, kq, mine, "prompt_own_half", after=(send,))
    (final_mine,) = whole(final_kernel, where, finals, [four], "final", after=(squares,))
    final_other = swap_cores(final_mine)
    prompt_out, token = finish(
        where, part, gate, kq, other, gated, squares, gain_row, 4, "prompt_finish", after=(final_mine,)
    )
    resp_gated, resp_squares = own_half(
        where, resp_part, resp_gate, resp_kq, final_mine, "resp_own_half", after=(token,)
    )
    resp_out, _ = finish(
        where, resp_part, resp_gate, resp_kq, final_other, resp_gated, resp_squares, gain_row, 5, "resp_finish",
        after=(token,),
    )
    return (prompt_out, resp_out[None])


def solution(mesh):
    return jax.shard_map(
        shards,
        mesh=mesh,
        in_specs=(
            P(("grp", "seq", "resp"), None),
            P(("grp", "seq", "resp"), None),
            P(None, ("grp", "seq", "resp")),
            P(None, ("grp", "seq", "resp")),
            P(("grp", "seq", "resp"), None, None),
            P(("grp", "seq", "resp"), None, None),
            P(None, ("grp", "seq", "resp"), None),
            P(None, ("grp", "seq", "resp"), None),
            P(("grp", "seq", "resp")),
            P(),
            P(),
            P(),
            P(),
        ),
        out_specs=(P(("grp", "seq", "resp"), None), P(("grp", "seq", "resp"), None, None)),
        check_vma=False,
    )
```
